256 devices in a mesh: lon: 64 (over z, x, core), lat: 4 (over y).
Axes of the slice: x: 4, y: 4, z: 8, core: 2. Of those that a mesh axis runs over, the one named last changes fastest.
Arguments:
- state: float32 [6, 32, 512, 512], P(None, None, 'lon', 'lat'), may hold values from -6 to 6
- cotangent: float32 [6, 32, 512, 512], P(None, None, 'lon', 'lat'), may hold values from -6 to 6
- active: int32 [32, 512, 512], P(None, 'lon', 'lat'), may hold values from 0 to 1, as said below
- wet: int32 [512, 512], P('lon', 'lat'), may hold values 0 or 1
- surface_diag: float32 [512, 512], P('lon', 'lat'), may hold values from 0.02 to 0.2
Outputs:
- state_adjoint: float32 [6, 32, 512, 512], P(None, None, 'lon', 'lat')
- surface_adjoint: float32 [512, 512], P('lon', 'lat')
The draws below stay inside these ranges and needn't reach their ends.
Inputs may be any that keep to these rules, and one draw needn't show every extreme that they name: 1 marks an active-ecosystem cell. `wet`: 1 marks a sea column.
All inputs are finite; a program needn't handle non-finite values. No bound on the sum of `wet` on one device may be relied on, other than what follows from the above.
Results may differ from the reference program's by a relative error of at most 0.0003.
Values sent between devices are 32-bit elements; how exact they have to be, the bound alone decides.
A program may use at most 64 MiB of HBM per device.

```python
import math
import jax
import jax.numpy as jnp

NTR = 6
NZ = 32
ITERS = 8
NX = 512
NY = 512


def draw_active(key, part):
    key = jax.random.fold_in(key, 7)
    first, second = jax.random.split(key)
    lat_index = jnp.arange(NY, dtype=jnp.int32)
    base = 2 + NZ * 3 // 4 * lat_index // NY
    jitter = jax.random.randint(first, (NX, NY), 0, NZ // 4 + 1)
    depth = jnp.minimum(base[None, :] + jitter, NZ)
    levels = jnp.arange(NZ, dtype=jnp.int32)[:, None, None]
    band = levels < depth[None, :, :]
    patchy = jax.random.randint(second, (NZ, NX, NY), 0, 4) > 0
    return jnp.where(band & patchy, 1, 0).astype(jnp.int32)


def set_ends(result, own_key, smallest, top_value):
    dims = result.shape
    index_at = [jax.random.randint(jax.random.fold_in(own_key, axis), (), 0, dims[axis]) for axis in range(len(dims))]
    result = result.at[tuple(index_at)].set(smallest)
    longest = dims.index(max(dims))
    index_at[longest] = (index_at[longest] + 1) % dims[longest]
    return result.at[tuple(index_at)].set(top_value)


def block_scale(rng, extent, shards, least, top_value):
    loudness, own = 1.0, jax.random.fold_in(rng, 6)
    for dim, shards_of in shards:
        heights = jnp.exp(jax.random.uniform(jax.random.fold_in(own, dim), (shards_of,), jnp.float32, least / len(shards), top_value / len(shards)))
        loudness = loudness * jnp.repeat(heights, extent[dim] // shards_of).reshape([-1 if axis == dim else 1 for axis in range(len(extent))])
    return loudness


def noise(rng, shape, deviation, most, pieces=(), held_as=jnp.bfloat16):
    drawn = deviation * jax.random.normal(rng, shape, jnp.float32)
    if pieces:
        drawn = drawn * block_scale(rng, shape, pieces, -0.22, 0.18)
    return jnp.clip(drawn, -most, most).astype(held_as)


def setup_inputs(seed: int = 0) -> dict:
    arg_keys = jax.random.split(jax.random.key(seed), 6)
    return {
        "state": noise(arg_keys[0], (NTR, NZ, NX, NY), 1.0, 6.0, ((2, 64), (3, 4)), jnp.float32),
        "cotangent": noise(arg_keys[1], (NTR, NZ, NX, NY), 1.0, 6.0, ((2, 64), (3, 4)), jnp.float32),
        "active": draw_active(jax.random.fold_in(arg_keys[5], 71), 0),
        "wet": set_ends((jax.random.randint(arg_keys[3], (NX, NY), 0, 10) < 9).astype(jnp.int32), jax.random.fold_in(arg_keys[3], 1), 0, 1),
        "surface_diag": jnp.clip(jnp.exp(math.log(0.2) - 2.3025851 * jax.random.uniform(arg_keys[4], (NX, NY), jnp.float32) ** block_scale(arg_keys[4], (NX, NY), ((0, 64), (1, 4)), -0.2, 0.2)), 0.02, 0.2),
    }


GRAV = (0.5, 0.4, -0.3, 0.2, 0.3, -0.4)
LOAD = (0.3, -0.2, 0.25, 0.15, -0.1, 0.2)
STOICH = (1.0, 0.5, -1.1, 0.3, 0.8, -0.6)


def pad_field(field):
    lead = ((0, 0),) * (field.ndim - 2)
    field = jnp.pad(field, lead + ((1, 1), (0, 0)), mode="wrap")
    return jnp.pad(field, lead + ((0, 0), (1, 1)))


def stencil(padded, mpad):
    center = padded[..., 1:-1, 1:-1]
    m = mpad[1:-1, 1:-1]
    total = m * mpad[2:, 1:-1] * (padded[..., 2:, 1:-1] - center)
    total = total + m * mpad[:-2, 1:-1] * (padded[..., :-2, 1:-1] - center)
    total = total + m * mpad[1:-1, 2:] * (padded[..., 1:-1, 2:] - center)
    total = total + m * mpad[1:-1, :-2] * (padded[..., 1:-1, :-2] - center)
    return total


def reference(state, cotangent, active, wet, surface_diag):
    mpad = pad_field(wet.astype(jnp.float32))
    mixed = state + 0.2 * stencil(pad_field(state), mpad)
    phyto = jnp.tanh(mixed[0])
    iron = mixed[1]
    limit = iron * iron / (1.0 + iron * iron)
    grav = jnp.array(GRAV, jnp.float32)[:, None, None, None]
    forcing = jnp.sum(grav * cotangent, axis=(0, 1)) / NZ

    def operate(field):
        return surface_diag * field - stencil(pad_field(field), mpad)

    solution = jnp.zeros_like(forcing)
    residual, direction = forcing, forcing
    norm_now = jnp.sum(residual * residual)
    for step in range(ITERS):
        image = operate(direction)
        alpha = norm_now / jnp.sum(direction * image)
        solution = solution + alpha * direction
        residual = residual - alpha * image
        norm_next = jnp.sum(residual * residual)
        direction = residual + (norm_next / norm_now) * direction
        norm_now = norm_next
    load = jnp.array(LOAD, jnp.float32)[:, None, None, None]
    after = cotangent + load * solution
    stoich = jnp.array(STOICH, jnp.float32)[:, None, None, None]
    uptake_adj = -jnp.sum(stoich * after, axis=0)
    act = active.astype(jnp.float32)
    factor = 0.8 * act * uptake_adj
    first = after[0] + factor * (1.0 - phyto * phyto) * limit
    denom = 1.0 + iron * iron
    second = after[1] + factor * phyto * 2.0 * iron / (denom * denom)
    before = jnp.concatenate([first[None], second[None], after[2:]], axis=0)
    state_adjoint = before + 0.2 * stencil(pad_field(before), mpad)
    return state_adjoint, solution
```

```python
import functools

import jax
import jax.numpy as jnp
from jax import lax
from jax.experimental import pallas as pl
from jax.experimental.pallas import tpu as pltpu
from jax.sharding import PartitionSpec as P

ITERS = 8


GRAV = (0.5, 0.4, -0.3, 0.2, 0.3, -0.4)
LOAD = (0.3, -0.2, 0.25, 0.15, -0.1, 0.2)
STOICH = (1.0, 0.5, -1.1, 0.3, 0.8, -0.6)
STOICH_LOAD = sum(s * w for s, w in zip(STOICH, LOAD))

CENTER = 4.11
HALF = 4.09
CONDITION = 1.0e5

MESH = pl.DeviceIdType.MESH


def with_halo(block, sides, width):
    for axis, dim in sides:
        count = lax.axis_size(axis)
        forward = [(i, i + 1) for i in range(count - 1)]
        forward.append((count - 1, 0))
        backward = [(target, source) for source, target in forward]
        low = lax.ppermute(
            lax.slice_in_dim(block, block.shape[dim] - width, None, axis=dim), axis, forward
        )
        high = lax.ppermute(lax.slice_in_dim(block, 0, width, axis=dim), axis, backward)
        block = jnp.concatenate([low, block, high], axis=dim)
    return block


def stencil(padded, mpad):
    center = padded[..., 1:-1, 1:-1]
    m = mpad[1:-1, 1:-1]
    total = m * mpad[2:, 1:-1] * (padded[..., 2:, 1:-1] - center)
    total = total + m * mpad[:-2, 1:-1] * (padded[..., :-2, 1:-1] - center)
    total = total + m * mpad[1:-1, 2:] * (padded[..., 1:-1, 2:] - center)
    total = total + m * mpad[1:-1, :-2] * (padded[..., 1:-1, :-2] - center)
    return total


def surface_operator(field, surface_diag, mpad):
    padded = with_halo(field, (("lon", 0), ("lat", 1)), 1)
    return surface_diag * field - stencil(padded, mpad)


def squares(residual):
    return lax.psum(jnp.sum(residual * residual), ("lon", "lat"))


def step_by_step(state, cotangent, active, wet, surface_diag):
    tracers, levels, rows, cols = state.shape
    wet_float = wet.astype(jnp.float32)
    stacked = jnp.concatenate(
        [state.reshape(tracers * levels, rows, cols), wet_float[None]], axis=0
    )
    padded = with_halo(stacked, (("lon", 1), ("lat", 2)), 1)
    lat_id = lax.axis_index("lat")
    lat_count = lax.axis_size("lat")
    edge = jnp.arange(cols + 2, dtype=jnp.int32)
    keep = jnp.where((edge == 0) & (lat_id == 0), 0.0, 1.0)
    keep = jnp.where((edge == cols + 1) & (lat_id == lat_count - 1), 0.0, keep).astype(jnp.float32)
    mpad = padded[-1] * keep[None, :]
    state_pad = padded[:-1].reshape(tracers, levels, rows + 2, cols + 2)
    mixed = state + 0.2 * stencil(state_pad, mpad)
    phyto = jnp.tanh(mixed[0])
    iron = mixed[1]
    limit = iron * iron / (1.0 + iron * iron)
    grav = jnp.array(GRAV, jnp.float32)[:, None, None, None]
    forcing = jnp.sum(grav * cotangent, axis=(0, 1)) / levels

    def iteration(_, carry):
        total, residual, direction, norm_now = carry
        image = surface_operator(direction, surface_diag, mpad)
        alpha = norm_now / lax.psum(jnp.sum(direction * image), ("lon", "lat"))
        total = total + alpha * direction
        residual = residual - alpha * image
        norm_next = squares(residual)
        direction = residual + norm_next / norm_now * direction
        return total, residual, direction, norm_next

    total, _, _, _ = lax.fori_loop(
        0, ITERS, iteration, (jnp.zeros_like(forcing), forcing, forcing, squares(forcing))
    )
    load = jnp.array(LOAD, jnp.float32)[:, None, None, None]
    after = cotangent + load * total
    stoich = jnp.array(STOICH, jnp.float32)[:, None, None, None]
    uptake_adj = -jnp.sum(stoich * after, axis=0)
    factor = 0.8 * active.astype(jnp.float32) * uptake_adj
    first = after[0] + factor * (1.0 - phyto * phyto) * limit
    denom = 1.0 + iron * iron
    second = after[1] + factor * phyto * 2.0 * iron / (denom * denom)
    before = jnp.concatenate([first[None], second[None], after[2:]], axis=0)
    spread = stencil(with_halo(before, (("lon", 2), ("lat", 3)), 1), mpad)
    return before + 0.2 * spread, total


def moment_solve(nu):
    gamma = 2.0 * CENTER / HALF
    zero = jnp.zeros_like(nu[0])
    size = ITERS + 1
    res, dirn = dict(enumerate(nu)), dict(enumerate(nu))
    r = [zero + 1.0] + [None] * (size - 1)
    d = [zero + 1.0] + [None] * (size - 1)
    x = [None] * size
    rr = nu[0]
    condition = zero
    least = rr
    for k in range(ITERS):
        top = 2 * ITERS - 1 - k
        image = {
            l: gamma * dirn[l] + (dirn[l + 1] + dirn[abs(l - 1)]) for l in range(k, top)
        }
        curvature = d[k] * image[k]
        inverse = 1.0 / curvature
        alpha = rr * inverse
        bulk = functools.reduce(lambda a, b: a + b, [jnp.abs(d[l]) for l in range(k + 1)])
        condition = condition + bulk * bulk * inverse
        least = jnp.minimum(least, curvature)
        for l in range(k + 1):
            step = alpha * d[l]
            x[l] = step if x[l] is None else x[l] + step
        if k == ITERS - 1:
            break
        for j in range(k + 2):
            terms = []
            if j > 0:
                terms.append(d[j - 1] * 2.0 if j == 1 else d[j - 1])
            if j + 1 <= k:
                terms.append(d[j + 1])
            if j <= k:
                terms.append(gamma * d[j])
            moved = alpha * functools.reduce(lambda a, b: a + b, terms)
            r[j] = -moved if r[j] is None else r[j] - moved
        res = {l: res[l] - alpha * image[l] for l in range(k + 1, top)}
        rr_next = r[k + 1] * res[k + 1]
        least = jnp.minimum(least, rr_next)
        beta = rr_next / rr
        d = [
            None if r[l] is None else (r[l] if d[l] is None else r[l] + beta * d[l])
            for l in range(size)
        ]
        new = {l: res[l] + beta * dirn[l] for l in range(k + 1, top)}
        new[k] = beta * dirn[k]
        dirn = new
        rr = rr_next
    good = (condition * nu[0] < CONDITION / 4.0) & (least > 0.0)
    return [v * (2.0 / HALF) for v in x[:ITERS]], good


def fused_kernel(
    lon_count,
    lat_count,
    levels,
    state_hbm,
    cot_hbm,
    active_hbm,
    wet_hbm,
    diag_hbm,
    out_hbm,
    sol_ref,
    good_ref,
    state_v,
    cot_v,
    active_v,
    wet_v,
    diag_v,
    out_v,
    q_v,
    g_v,
    shift_v,
    basis_v,
    near_v,
    coef_v,
    row_send,
    row_recv,
    qrow_send,
    qrow_recv,
    col_send,
    col_recv,
    qcol_send,
    qcol_recv,
    col_v,
    sum_a,
    sum_b,
    in_sems,
    out_sems,
    send_sems,
    recv_sems,
):
    rows, cols = 8, 128
    planes = 2 * levels
    lon = lax.axis_index("lon")
    lat = lax.axis_index("lat")
    inner = min(8, lon_count)
    z, x, core = lon // inner, lax.rem(lon, inner) // 2, lax.rem(lon, 2)

    copies = [
        pltpu.make_async_copy(src, dst, in_sems.at[i])
        for i, (src, dst) in enumerate(
            (
                (wet_hbm, wet_v),
                (diag_hbm, diag_v),
                (cot_hbm, cot_v),
                (state_hbm.at[pl.ds(0, planes * rows)], state_v),
                (active_hbm, active_v),
            )
        )
    ]
    for copy in copies:
        copy.start()

    def neighbour(dlon, dlat):
        return (
            lax.rem(lon + (dlon + lon_count), lon_count),
            lax.rem(lat + (dlat + lat_count), lat_count),
        )

    around = [(i, j) for i in (-1, 0, 1) for j in (-1, 0, 1) if (i, j) != (0, 0)]
    count_a = 2 * (lon_count // inner)
    count_b = (inner // 2) * lat_count
    index_a = z * 2 + core
    index_b = x * lat_count + lat

    def partner_a(step):
        j = lax.rem(index_a + step, count_a)
        return ((j // 2) * inner + x * 2 + lax.rem(j, 2), lat)

    def partner_b(step):
        j = lax.rem(index_b + step, count_b)
        return (z * inner + (j // lat_count) * 2 + core, lax.rem(j, lat_count))

    partners = [neighbour(i, j) for i, j in around if i != 0]
    partners += [partner_a(s) for s in range(1, count_a)]
    partners += [partner_b(s) for s in range(1, count_b)]
    barrier = pltpu.get_barrier_semaphore()
    for partner in partners:
        pl.semaphore_signal(barrier, inc=1, device_id=partner, device_id_type=MESH)

    lane = lax.broadcasted_iota(jnp.int32, (rows, cols), 1)
    sub = lax.broadcasted_iota(jnp.int32, (rows, cols), 0)
    even = lax.rem(lane, 2) == 0
    first_lane, last_lane = lane == 0, lane == cols - 1
    first_sub, last_sub = sub == 0, sub == rows - 1
    keep_low = jnp.where(lat == 0, 0.0, 1.0).astype(jnp.float32)
    keep_high = jnp.where(lat == lat_count - 1, 0.0, 1.0).astype(jnp.float32)

    def tile(ref, index):
        start = index * rows
        if not isinstance(start, int):
            start = pl.multiple_of(start, rows)
        return ref[pl.ds(start, rows), :]

    def put(ref, index, value):
        start = index * rows
        if not isinstance(start, int):
            start = pl.multiple_of(start, rows)
        ref[pl.ds(start, rows), :] = value

    def spread_row(ref, index):
        return jnp.broadcast_to(ref[pl.ds(index, 1), :], (rows, cols))

    copies[0].wait()
    copies[1].wait()
    m = wet_v[...].astype(jnp.float32)
    near_v[4, pl.ds(0, rows), :] = m
    near_v[4, pl.ds(rows, rows), :] = diag_v[...]
    copies[2].wait()
    tracers = len(GRAV)
    unroll = 4

    def add_levels(i, acc):
        acc = list(acc)
        for u in range(unroll):
            for t in range(tracers):
                acc[t] = acc[t] + tile(cot_v, t * levels + i * unroll + u)
        return tuple(acc)

    acc = lax.fori_loop(
        0, levels // unroll, add_levels, (jnp.zeros((rows, cols), jnp.float32),) * tracers
    )
    forcing = functools.reduce(lambda a, b: a + b, [g * v for g, v in zip(GRAV, acc)])
    near_v[4, pl.ds(2 * rows, rows), :] = forcing * (1.0 / levels)

    pl.semaphore_wait(barrier, len(partners))
    for dlon, dlat in around:
        pltpu.make_async_remote_copy(
            src_ref=near_v.at[4],
            dst_ref=near_v.at[(1 - dlon) * 3 + (1 - dlat)],
            send_sem=send_sems.at[0],
            recv_sem=recv_sems.at[0],
            device_id=neighbour(dlon, dlat),
            device_id_type=MESH,
        ).start()

    low, high = neighbour(-1, 0), neighbour(1, 0)
    west, east = neighbour(0, -1), neighbour(0, 1)

    def send(src, dst, sem, device):
        copy = pltpu.make_async_remote_copy(
            src_ref=src,
            dst_ref=dst,
            send_sem=send_sems.at[sem],
            recv_sem=recv_sems.at[sem],
            device_id=device,
            device_id_type=MESH,
        )
        copy.start()
        return copy

    copies[3].wait()
    m_first, m_last = m[0:1, :], m[rows - 1 : rows, :]
    total = tracers * levels
    row_send[0, pl.ds(0, planes), :] = state_v[pl.ds(0, planes, stride=rows), :] * m_first
    row_send[1, pl.ds(0, planes), :] = state_v[pl.ds(rows - 1, planes, stride=rows), :] * m_last
    row_send[0, pl.ds(planes, total), :] = cot_v[pl.ds(0, total, stride=rows), :] * m_first
    row_send[1, pl.ds(planes, total), :] = cot_v[pl.ds(rows - 1, total, stride=rows), :] * m_last
    sent_rows = [
        send(row_send.at[0], row_recv.at[1], 1, low),
        send(row_send.at[1], row_recv.at[0], 2, high),
    ]

    m_edges = jnp.where(even, m[:, cols - 1 : cols], m[:, 0:1])
    half = lane // 2
    pack_unroll = 8

    def pack(ref, base):
        def some(i, packed):
            for u in range(pack_unroll):
                p = i * pack_unroll + u
                moved = pltpu.roll(tile(ref, base + p), 2 * p + 1, 1)
                packed = jnp.where(half == p, moved, packed)
            return packed

        packed = lax.fori_loop(
            0, planes // pack_unroll, some, jnp.zeros((rows, cols), jnp.float32)
        )
        return packed * m_edges

    put(col_send, 0, pack(state_v, 0))
    for g in range(tracers // 2):
        put(col_send, g + 1, pack(cot_v, g * planes))
    sent_cols = [
        send(col_send, col_recv.at[1], 3, west),
        send(col_send, col_recv.at[0], 4, east),
    ]

    def joined(from_west, from_east):
        return jnp.where(
            even,
            pltpu.roll(from_east, cols - 1, 1) * keep_high,
            pltpu.roll(from_west, 1, 1) * keep_low,
        )

    pltpu.make_async_copy(
        near_v.at[pl.ds(0, 8)], near_v.at[pl.ds(0, 8)], recv_sems.at[0]
    ).wait()

    def field(part, low_edge=None, high_edge=None):
        tiles = []
        for i in range(3):
            block = [near_v[i * 3 + j, pl.ds(part * rows, rows), :] for j in range(3)]
            left = block[0] if low_edge is None else block[0] * low_edge
            right = block[2] if high_edge is None else block[2] * high_edge
            tiles.append([block[1], jnp.where(lane < cols // 2, right, left)])
        return tiles

    def shifts(tiles):
        plus = [[pltpu.roll(v, 1, 1) for v in pair] for pair in tiles]
        minus = [[pltpu.roll(v, cols - 1, 1) for v in pair] for pair in tiles]
        below = [[pltpu.roll(v, 1, 0) for v in pair] for pair in tiles]
        above = [[pltpu.roll(v, rows - 1, 0) for v in pair] for pair in tiles]
        result = []
        for i in range(3):
            pair = []
            for j in range(2):
                pair.append(
                    (
                        jnp.where(first_lane, plus[i][1 - j], plus[i][j]),
                        jnp.where(last_lane, minus[i][1 - j], minus[i][j]),
                        jnp.where(first_sub, below[(i + 2) % 3][j], below[i][j]),
                        jnp.where(last_sub, above[(i + 1) % 3][j], above[i][j]),
                    )
                )
            result.append(pair)
        return result

    def add4(four):
        return (four[0] + four[1]) + (four[2] + four[3])

    cells = [(i, j) for i in range(3) for j in range(2)]

    def each(function):
        return [[function(i, j) for j in range(2)] for i in range(3)]

    mask = field(0, keep_low, keep_high)
    mask_shift = shifts(mask)
    degree = each(lambda i, j: mask[i][j] * add4(mask_shift[i][j]))
    diag = field(1)
    on_self = each(lambda i, j: (2.0 / HALF) * (diag[i][j] + degree[i][j] - CENTER))
    on_near = each(lambda i, j: (2.0 / HALF) * mask[i][j])
    mixing_self = 1.0 - 0.2 * degree[1][0]
    mixing_near = 0.2 * m
    coef_v[pl.ds(0, rows), :] = mixing_self

    kept = [(1, 0), (1, 1), (0, 0), (2, 0)]

    def keep(k, tiles):
        for n, (i, j) in enumerate(kept):
            put(basis_v, k * len(kept) + n, tiles[i][j])

    def twice(tiles):
        moved = shifts(each(lambda i, j: mask[i][j] * tiles[i][j]))
        return each(lambda i, j: on_self[i][j] * tiles[i][j] - on_near[i][j] * add4(moved[i][j]))

    def row_sum(a, b):
        return jnp.sum(a * b, axis=0, keepdims=True)

    now = field(2)
    keep(0, now)
    doubled = twice(now)
    later = each(lambda i, j: 0.5 * doubled[i][j])
    sums = [row_sum(now[1][0], now[1][0]), row_sum(now[1][0], later[1][0])]
    for k in range(1, ITERS):
        keep(k, later)
        doubled = twice(later)
        before = now
        now = later
        later = each(lambda i, j: doubled[i][j] - before[i][j])
        sums.append(row_sum(now[1][0], now[1][0]))
        sums.append(row_sum(now[1][0], later[1][0]))

    row = jnp.zeros((1, cols), jnp.float32)
    for part in range(2 * ITERS // rows):
        stacked = jnp.concatenate(sums[part * rows : (part + 1) * rows], axis=0)
        spread = jnp.broadcast_to(jnp.sum(stacked, axis=1, keepdims=True), (rows, cols))
        row = row + jnp.sum(
            jnp.where(lane == sub + part * rows, spread, 0.0), axis=0, keepdims=True
        )

    def exchange(buffer, index, count, partner, sem):
        for step in range(1, count):
            send(buffer.at[index], buffer.at[index], sem, partner(step))

    def collect(buffer, count, sem):
        part = buffer.at[pl.ds(0, count - 1)]
        pltpu.make_async_copy(part, part, recv_sems.at[sem]).wait()
        values = [buffer[i] for i in range(count)]
        while len(values) > 1:
            values = [
                values[i] + values[i + 1] if i + 1 < len(values) else values[i]
                for i in range(0, len(values), 2)
            ]
        return values[0]

    sum_a[index_a] = row
    exchange(sum_a, index_a, count_a, partner_a, 5)

    for copy in sent_rows:
        copy.wait_recv()
    for copy in sent_cols:
        copy.wait_recv()
    for g in range(1 + tracers // 2):
        put(
            col_v,
            g,
            joined(
                col_recv[0, pl.ds(g * rows, rows), :], col_recv[1, pl.ds(g * rows, rows), :]
            ),
        )

    def four_around(value, below_row, above_row, columns, index):
        held = m * value
        sides = pltpu.roll(columns, cols - 1 - 2 * index, 1)
        return (
            jnp.where(first_lane, sides, pltpu.roll(held, 1, 1)),
            jnp.where(last_lane, sides, pltpu.roll(held, cols - 1, 1)),
            jnp.where(first_sub, below_row, pltpu.roll(held, 1, 0)),
            jnp.where(last_sub, above_row, pltpu.roll(held, rows - 1, 0)),
        )

    def mixing(value, below_row, above_row, columns, index):
        near = add4(four_around(value, below_row, above_row, columns, index))
        return mixing_self * value + mixing_near * near

    copies[4].wait()
    columns_state = tile(col_v, 0)

    def uptake(i, carry):
        for u in range(2):
            level = i * 2 + u
            mixed = [
                mixing(
                    tile(state_v, t * levels + level),
                    spread_row(row_recv.at[0], t * levels + level),
                    spread_row(row_recv.at[1], t * levels + level),
                    columns_state,
                    t * levels + level,
                )
                for t in range(2)
            ]
            phyto, iron = jnp.tanh(mixed[0]), mixed[1]
            squared = iron * iron
            inverse = 1.0 / (1.0 + squared)
            factor = -0.8 * tile(active_v, level).astype(jnp.float32)
            q0 = factor * (1.0 - phyto * phyto) * (squared * inverse)
            q1 = factor * phyto * (2.0 * iron) * (inverse * inverse)
            cot = [tile(cot_v, t * levels + level) for t in range(tracers)]
            mixture = functools.reduce(lambda a, b: a + b, [s * v for s, v in zip(STOICH, cot)])
            put(q_v, level, q0)
            put(q_v, levels + level, q1)
            put(g_v, level, cot[0] + q0 * mixture)
            put(g_v, levels + level, cot[1] + q1 * mixture)
        return carry

    lax.fori_loop(0, levels // 2, uptake, 0)
    qrow_send[0] = q_v[pl.ds(0, planes, stride=rows), :] * m_first
    qrow_send[1] = q_v[pl.ds(rows - 1, planes, stride=rows), :] * m_last
    put(qcol_send, 0, pack(q_v, 0))
    sent_q = [
        send(qrow_send.at[0], qrow_recv.at[1], 7, low),
        send(qrow_send.at[1], qrow_recv.at[0], 8, high),
        send(qcol_send, qcol_recv.at[1], 9, west),
        send(qcol_send, qcol_recv.at[0], 10, east),
    ]

    sum_b[index_b] = collect(sum_a, count_a, 5)
    exchange(sum_b, index_b, count_b, partner_b, 6)

    columns_cot = [tile(col_v, g + 1) for g in range(tracers // 2)]

    def plain(level, carry):
        for t in range(2, tracers):
            p = t * levels + level
            put(
                out_v,
                p,
                mixing(
                    tile(cot_v, p),
                    spread_row(row_recv.at[0], planes + p),
                    spread_row(row_recv.at[1], planes + p),
                    columns_cot[t // 2],
                    (t % 2) * levels + level,
                ),
            )
        return carry

    lax.fori_loop(0, levels, plain, 0)

    for copy in sent_q:
        copy.wait_recv()
    columns_q = joined(qcol_recv[0], qcol_recv[1])
    weighted = functools.reduce(
        lambda a, b: a + b,
        [
            jnp.where(lane < cols // 2, STOICH[2 * g], STOICH[2 * g + 1]) * columns_cot[g]
            for g in range(tracers // 2)
        ],
    )
    columns_g = columns_cot[0] + columns_q * (weighted + pltpu.roll(weighted, cols // 2, 1))
    for side in range(2):
        mixture = functools.reduce(
            lambda a, b: a + b,
            [
                STOICH[t] * row_recv[side, pl.ds(planes + t * levels, levels), :]
                for t in range(tracers)
            ],
        )
        for t in range(2):
            where = pl.ds(planes + t * levels, levels)
            row_send_part = row_recv[side, where, :]
            row_recv[side, where, :] = (
                row_send_part + qrow_recv[side, pl.ds(t * levels, levels), :] * mixture
            )

    def changed(level, carry):
        for t in range(2):
            p = t * levels + level
            put(
                out_v,
                p,
                mixing(
                    tile(g_v, p),
                    spread_row(row_recv.at[0], planes + p),
                    spread_row(row_recv.at[1], planes + p),
                    columns_g,
                    p,
                ),
            )
            q = tile(q_v, p)
            four = four_around(
                q,
                spread_row(qrow_recv.at[0], p),
                spread_row(qrow_recv.at[1], p),
                columns_q,
                p,
            )
            put(shift_v, p * 5, (STOICH_LOAD * mixing_self) * q)
            for n in range(4):
                put(shift_v, p * 5 + 1 + n, (STOICH_LOAD * mixing_near) * four[n])
        return carry

    lax.fori_loop(0, levels, changed, 0)

    totals = jnp.broadcast_to(collect(sum_b, count_b, 6), (rows, cols))
    inner_sums = []
    for part in range(2 * ITERS // rows):
        chosen = jnp.sum(
            jnp.where(lane == sub + part * rows, totals, 0.0), axis=1, keepdims=True
        )
        chosen = jnp.broadcast_to(chosen, (rows, cols))
        inner_sums += [
            jnp.broadcast_to(chosen[i : i + 1, :], (rows, cols)) for i in range(rows)
        ]
    nu = [inner_sums[0], inner_sums[1]]
    for k in range(1, ITERS):
        nu.append(2.0 * inner_sums[2 * k] - inner_sums[0])
        nu.append(2.0 * inner_sums[2 * k + 1] - inner_sums[1])
    weights, good = moment_solve(nu)

    solved = {}
    for n, cell in enumerate(kept):
        solved[cell] = functools.reduce(
            lambda a, b: a + b,
            [weights[k] * tile(basis_v, k * len(kept) + n) for k in range(ITERS)],
        )
    own = solved[(1, 0)]
    sol_ref[...] = own
    good_ref[0] = jnp.where(good, 1, 0).astype(jnp.int32)[0, 0]
    held = {cell: mask[cell[0]][cell[1]] * solved[cell] for cell in kept}
    around_x = (
        jnp.where(first_lane, pltpu.roll(held[(1, 1)], 1, 1), pltpu.roll(held[(1, 0)], 1, 1)),
        jnp.where(
            last_lane,
            pltpu.roll(held[(1, 1)], cols - 1, 1),
            pltpu.roll(held[(1, 0)], cols - 1, 1),
        ),
        jnp.where(first_sub, pltpu.roll(held[(0, 0)], 1, 0), pltpu.roll(held[(1, 0)], 1, 0)),
        jnp.where(
            last_sub,
            pltpu.roll(held[(2, 0)], rows - 1, 0),
            pltpu.roll(held[(1, 0)], rows - 1, 0),
        ),
    )
    spread_x = mixing_self * own + mixing_near * add4(around_x)

    written = []
    for t in (2, 3, 4, 5, 0, 1):
        added = LOAD[t] * spread_x

        def finish(i, carry, t=t, added=added):
            for u in range(unroll):
                p = t * levels + i * unroll + u
                value = tile(out_v, p) + added
                if t < 2:
                    value = value + tile(shift_v, p * 5) * own
                    for n in range(4):
                        value = value + tile(shift_v, p * 5 + 1 + n) * around_x[n]
                put(out_v, p, value)
            return carry

        lax.fori_loop(0, levels // unroll, finish, 0)
        where = pl.ds(t * levels * rows, levels * rows)
        copy = pltpu.make_async_copy(out_v.at[where], out_hbm.at[where], out_sems.at[t])
        copy.start()
        written.append(copy)

    pltpu.make_async_copy(
        near_v.at[pl.ds(0, 8)], near_v.at[pl.ds(0, 8)], send_sems.at[0]
    ).wait()
    for copy in sent_rows + sent_cols + sent_q:
        copy.wait_send()
    for buffer, count, sem in ((sum_a, count_a, 5), (sum_b, count_b, 6)):
        part = buffer.at[pl.ds(0, count - 1)]
        pltpu.make_async_copy(part, part, send_sems.at[sem]).wait()
    for copy in written:
        copy.wait()


def on_device(state, cotangent, active, wet, surface_diag):
    tracers, levels, rows, cols = state.shape
    lon_count, lat_count = lax.axis_size("lon"), lax.axis_size("lat")
    total = tracers * levels
    planes = 2 * levels
    inner = min(8, lon_count)
    f32 = jnp.float32
    anywhere = pl.BlockSpec(memory_space=pl.ANY)
    out, sol, good = pl.pallas_call(
        functools.partial(fused_kernel, lon_count, lat_count, levels),
        out_shape=(
            jax.ShapeDtypeStruct((total * rows, cols), f32),
            jax.ShapeDtypeStruct((rows, cols), f32),
            jax.ShapeDtypeStruct((1,), jnp.int32),
        ),
        in_specs=[anywhere] * 5,
        out_specs=(
            anywhere,
            pl.BlockSpec(memory_space=pltpu.VMEM),
            pl.BlockSpec(memory_space=pltpu.SMEM),
        ),
        scratch_shapes=[
            pltpu.VMEM((planes * rows, cols), f32),
            pltpu.VMEM((total * rows, cols), f32),
            pltpu.VMEM((levels * rows, cols), jnp.int32),
            pltpu.VMEM((rows, cols), jnp.int32),
            pltpu.VMEM((rows, cols), f32),
            pltpu.VMEM((total * rows, cols), f32),
            pltpu.VMEM((planes * rows, cols), f32),
            pltpu.VMEM((planes * rows, cols), f32),
            pltpu.VMEM((planes * 5 * rows, cols), f32),
            pltpu.VMEM((ITERS * 4 * rows, cols), f32),
            pltpu.VMEM((9, 3 * rows, cols), f32),
            pltpu.VMEM((rows, cols), f32),
            pltpu.VMEM((2, planes + total, cols), f32),
            pltpu.VMEM((2, planes + total, cols), f32),
            pltpu.VMEM((2, planes, cols), f32),
            pltpu.VMEM((2, planes, cols), f32),
            pltpu.VMEM(((1 + tracers // 2) * rows, cols), f32),
            pltpu.VMEM((2, (1 + tracers // 2) * rows, cols), f32),
            pltpu.VMEM((rows, cols), f32),
            pltpu.VMEM((2, rows, cols), f32),
            pltpu.VMEM(((1 + tracers // 2) * rows, cols), f32),
            pltpu.VMEM((2 * (lon_count // inner), 1, cols), f32),
            pltpu.VMEM(((inner // 2) * lat_count, 1, cols), f32),
            pltpu.SemaphoreType.DMA((5,)),
            pltpu.SemaphoreType.DMA((tracers,)),
            pltpu.SemaphoreType.DMA((11,)),
            pltpu.SemaphoreType.DMA((11,)),
        ],
        compiler_params=pltpu.CompilerParams(
            collective_id=0, has_side_effects=True, vmem_limit_bytes=32 * 1024 * 1024
        ),
        name="fused_step",
    )(
        state.reshape(total * rows, cols),
        cotangent.reshape(total * rows, cols),
        active.reshape(levels * rows, cols),
        wet,
        surface_diag,
    )
    out = out.reshape(state.shape)
    return lax.cond(
        good[0] > 0,
        lambda *_: (out, sol),
        step_by_step,
        state,
        cotangent,
        active,
        wet,
        surface_diag,
    )


def solution(mesh):
    return jax.shard_map(
        on_device,
        mesh=mesh,
        in_specs=(
            P(None, None, "lon", "lat"),
            P(None, None, "lon", "lat"),
            P(None, "lon", "lat"),
            P("lon", "lat"),
            P("lon", "lat"),
        ),
        out_specs=(P(None, None, "lon", "lat"), P("lon", "lat")),
        check_vma=False,
    )
```

```python
import functools

import jax
import jax.numpy as jnp
from jax import lax
from jax.experimental import pallas as pl
from jax.experimental.pallas import tpu as pltpu
from jax.sharding import PartitionSpec as P

ITERS = 8


GRAV = (0.5, 0.4, -0.3, 0.2, 0.3, -0.4)
LOAD = (0.3, -0.2, 0.25, 0.15, -0.1, 0.2)
STOICH = (1.0, 0.5, -1.1, 0.3, 0.8, -0.6)
STOICH_LOAD = sum(s * w for s, w in zip(STOICH, LOAD))

CENTER = 4.11
HALF = 4.09
CONDITION = 1.0e5

MESH = pl.DeviceIdType.MESH


def with_halo(block, sides, width):
    for axis, dim in sides:
        count = lax.axis_size(axis)
        forward = [(i, i + 1) for i in range(count - 1)]
        forward.append((count - 1, 0))
        backward = [(target, source) for source, target in forward]
        low = lax.ppermute(
            lax.slice_in_dim(block, block.shape[dim] - width, None, axis=dim), axis, forward
        )
        high = lax.ppermute(lax.slice_in_dim(block, 0, width, axis=dim), axis, backward)
        block = jnp.concatenate([low, block, high], axis=dim)
    return block


def stencil(padded, mpad):
    center = padded[..., 1:-1, 1:-1]
    m = mpad[1:-1, 1:-1]
    total = m * mpad[2:, 1:-1] * (padded[..., 2:, 1:-1] - center)
    total = total + m * mpad[:-2, 1:-1] * (padded[..., :-2, 1:-1] - center)
    total = total + m * mpad[1:-1, 2:] * (padded[..., 1:-1, 2:] - center)
    total = total + m * mpad[1:-1, :-2] * (padded[..., 1:-1, :-2] - center)
    return total


def surface_operator(field, surface_diag, mpad):
    padded = with_halo(field, (("lon", 0), ("lat", 1)), 1)
    return surface_diag * field - stencil(padded, mpad)


def squares(residual):
    return lax.psum(jnp.sum(residual * residual), ("lon", "lat"))


def step_by_step(found, wet, surface_diag):
    rows, cols = wet.shape
    forcing = found[6 * rows :]
    mpad = with_halo(wet.astype(jnp.float32), (("lon", 0), ("lat", 1)), 1)
    lat_id = lax.axis_index("lat")
    lat_count = lax.axis_size("lat")
    edge = jnp.arange(cols + 2, dtype=jnp.int32)
    keep = jnp.where((edge == 0) & (lat_id == 0), 0.0, 1.0)
    keep = jnp.where((edge == cols + 1) & (lat_id == lat_count - 1), 0.0, keep).astype(jnp.float32)
    mpad = mpad * keep[None, :]

    def iteration(_, carry):
        total, residual, direction, norm_now = carry
        image = surface_operator(direction, surface_diag, mpad)
        alpha = norm_now / lax.psum(jnp.sum(direction * image), ("lon", "lat"))
        total = total + alpha * direction
        residual = residual - alpha * image
        norm_next = squares(residual)
        direction = residual + norm_next / norm_now * direction
        return total, residual, direction, norm_next

    total, _, _, _ = lax.fori_loop(
        0, ITERS, iteration, (jnp.zeros_like(forcing), forcing, forcing, squares(forcing))
    )
    padded = with_halo(total, (("lon", 0), ("lat", 1)), 1)
    spread = total + 0.2 * stencil(padded, mpad)
    held = mpad * padded
    return jnp.concatenate(
        [
            total,
            held[1:-1, :-2],
            held[1:-1, 2:],
            held[:-2, 1:-1],
            held[2:, 1:-1],
            spread,
            forcing,
        ],
        axis=0,
    )


def moment_solve(nu):
    gamma = 2.0 * CENTER / HALF
    zero = jnp.zeros_like(nu[0])
    size = ITERS + 1
    res, dirn = dict(enumerate(nu)), dict(enumerate(nu))
    r = [zero + 1.0] + [None] * (size - 1)
    d = [zero + 1.0] + [None] * (size - 1)
    x = [None] * size
    rr = nu[0]
    condition = zero
    least = rr
    for k in range(ITERS):
        top = 2 * ITERS - 1 - k
        image = {
            l: gamma * dirn[l] + (dirn[l + 1] + dirn[abs(l - 1)]) for l in range(k, top)
        }
        curvature = d[k] * image[k]
        inverse = 1.0 / curvature
        alpha = rr * inverse
        bulk = functools.reduce(lambda a, b: a + b, [jnp.abs(d[l]) for l in range(k + 1)])
        condition = condition + bulk * bulk * inverse
        least = jnp.minimum(least, curvature)
        for l in range(k + 1):
            step = alpha * d[l]
            x[l] = step if x[l] is None else x[l] + step
        if k == ITERS - 1:
            break
        for j in range(k + 2):
            terms = []
            if j > 0:
                terms.append(d[j - 1] * 2.0 if j == 1 else d[j - 1])
            if j + 1 <= k:
                terms.append(d[j + 1])
            if j <= k:
                terms.append(gamma * d[j])
            moved = alpha * functools.reduce(lambda a, b: a + b, terms)
            r[j] = -moved if r[j] is None else r[j] - moved
        res = {l: res[l] - alpha * image[l] for l in range(k + 1, top)}
        rr_next = r[k + 1] * res[k + 1]
        least = jnp.minimum(least, rr_next)
        beta = rr_next / rr
        d = [
            None if r[l] is None else (r[l] if d[l] is None else r[l] + beta * d[l])
            for l in range(size)
        ]
        new = {l: res[l] + beta * dirn[l] for l in range(k + 1, top)}
        new[k] = beta * dirn[k]
        dirn = new
        rr = rr_next
    good = (condition * nu[0] < CONDITION / 4.0) & (least > 0.0)
    return [v * (2.0 / HALF) for v in x[:ITERS]], good


def fused_kernel(
    lon_count,
    lat_count,
    levels,
    state_hbm,
    cot_hbm,
    active_hbm,
    wet_hbm,
    diag_hbm,
    out_v,
    shift_v,
    found_ref,
    good_ref,
    state_v,
    cot_v,
    active_v,
    wet_v,
    diag_v,
    q_v,
    g_v,
    basis_v,
    near_v,
    row_send,
    row_recv,
    qrow_send,
    qrow_recv,
    col_send,
    col_recv,
    qcol_send,
    qcol_recv,
    col_v,
    sum_a,
    sum_b,
    in_sems,
    send_sems,
    recv_sems,
):
    rows, cols = 8, 128
    planes = 2 * levels
    lon = lax.axis_index("lon")
    lat = lax.axis_index("lat")
    inner = min(8, lon_count)
    z, x, core = lon // inner, lax.rem(lon, inner) // 2, lax.rem(lon, 2)

    copies = [
        pltpu.make_async_copy(src, dst, in_sems.at[i])
        for i, (src, dst) in enumerate(
            (
                (wet_hbm, wet_v),
                (diag_hbm, diag_v),
                (cot_hbm, cot_v),
                (state_hbm.at[pl.ds(0, planes * rows)], state_v),
                (active_hbm, active_v),
            )
        )
    ]
    for copy in copies:
        copy.start()

    def neighbour(dlon, dlat):
        return (
            lax.rem(lon + (dlon + lon_count), lon_count),
            lax.rem(lat + (dlat + lat_count), lat_count),
        )

    around = [(i, j) for i in (-1, 0, 1) for j in (-1, 0, 1) if (i, j) != (0, 0)]
    count_a = 2 * (lon_count // inner)
    count_b = (inner // 2) * lat_count
    index_a = z * 2 + core
    index_b = x * lat_count + lat

    def partner_a(step):
        j = lax.rem(index_a + step, count_a)
        return ((j // 2) * inner + x * 2 + lax.rem(j, 2), lat)

    def partner_b(step):
        j = lax.rem(index_b + step, count_b)
        return (z * inner + (j // lat_count) * 2 + core, lax.rem(j, lat_count))

    partners = [neighbour(i, j) for i, j in around if i != 0]
    partners += [partner_a(s) for s in range(1, count_a)]
    partners += [partner_b(s) for s in range(1, count_b)]
    barrier = pltpu.get_barrier_semaphore()
    for partner in partners:
        pl.semaphore_signal(barrier, inc=1, device_id=partner, device_id_type=MESH)

    lane = lax.broadcasted_iota(jnp.int32, (rows, cols), 1)
    sub = lax.broadcasted_iota(jnp.int32, (rows, cols), 0)
    even = lax.rem(lane, 2) == 0
    first_lane, last_lane = lane == 0, lane == cols - 1
    first_sub, last_sub = sub == 0, sub == rows - 1
    keep_low = jnp.where(lat == 0, 0.0, 1.0).astype(jnp.float32)
    keep_high = jnp.where(lat == lat_count - 1, 0.0, 1.0).astype(jnp.float32)

    def tile(ref, index):
        start = index * rows
        if not isinstance(start, int):
            start = pl.multiple_of(start, rows)
        return ref[pl.ds(start, rows), :]

    def put(ref, index, value):
        start = index * rows
        if not isinstance(start, int):
            start = pl.multiple_of(start, rows)
        ref[pl.ds(start, rows), :] = value

    def spread_row(ref, index):
        return jnp.broadcast_to(ref[pl.ds(index, 1), :], (rows, cols))

    copies[0].wait()
    copies[1].wait()
    m = wet_v[...].astype(jnp.float32)
    near_v[4, pl.ds(0, rows), :] = m
    near_v[4, pl.ds(rows, rows), :] = diag_v[...]
    copies[2].wait()
    tracers = len(GRAV)
    unroll = 4

    def add_levels(i, acc):
        acc = list(acc)
        for u in range(unroll):
            for t in range(tracers):
                acc[t] = acc[t] + tile(cot_v, t * levels + i * unroll + u)
        return tuple(acc)

    acc = lax.fori_loop(
        0, levels // unroll, add_levels, (jnp.zeros((rows, cols), jnp.float32),) * tracers
    )
    forcing = functools.reduce(lambda a, b: a + b, [g * v for g, v in zip(GRAV, acc)])
    forcing = forcing * (1.0 / levels)
    near_v[4, pl.ds(2 * rows, rows), :] = forcing
    put(found_ref, 6, forcing)

    pl.semaphore_wait(barrier, len(partners))
    for dlon, dlat in around:
        pltpu.make_async_remote_copy(
            src_ref=near_v.at[4],
            dst_ref=near_v.at[(1 - dlon) * 3 + (1 - dlat)],
            send_sem=send_sems.at[0],
            recv_sem=recv_sems.at[0],
            device_id=neighbour(dlon, dlat),
            device_id_type=MESH,
        ).start()

    low, high = neighbour(-1, 0), neighbour(1, 0)
    west, east = neighbour(0, -1), neighbour(0, 1)

    def send(src, dst, sem, device):
        copy = pltpu.make_async_remote_copy(
            src_ref=src,
            dst_ref=dst,
            send_sem=send_sems.at[sem],
            recv_sem=recv_sems.at[sem],
            device_id=device,
            device_id_type=MESH,
        )
        copy.start()
        return copy

    copies[3].wait()
    m_first, m_last = m[0:1, :], m[rows - 1 : rows, :]
    total = tracers * levels
    row_send[0, pl.ds(0, planes), :] = state_v[pl.ds(0, planes, stride=rows), :] * m_first
    row_send[1, pl.ds(0, planes), :] = state_v[pl.ds(rows - 1, planes, stride=rows), :] * m_last
    row_send[0, pl.ds(planes, total), :] = cot_v[pl.ds(0, total, stride=rows), :] * m_first
    row_send[1, pl.ds(planes, total), :] = cot_v[pl.ds(rows - 1, total, stride=rows), :] * m_last
    sent_rows = [
        send(row_send.at[0], row_recv.at[1], 1, low),
        send(row_send.at[1], row_recv.at[0], 2, high),
    ]

    m_edges = jnp.where(even, m[:, cols - 1 : cols], m[:, 0:1])
    half = lane // 2
    pack_unroll = 8

    def pack(ref, base):
        def some(i, packed):
            for u in range(pack_unroll):
                p = i * pack_unroll + u
                moved = pltpu.roll(tile(ref, base + p), 2 * p + 1, 1)
                packed = jnp.where(half == p, moved, packed)
            return packed

        packed = lax.fori_loop(
            0, planes // pack_unroll, some, jnp.zeros((rows, cols), jnp.float32)
        )
        return packed * m_edges

    put(col_send, 0, pack(state_v, 0))
    for g in range(tracers // 2):
        put(col_send, g + 1, pack(cot_v, g * planes))
    sent_cols = [
        send(col_send, col_recv.at[1], 3, west),
        send(col_send, col_recv.at[0], 4, east),
    ]

    def joined(from_west, from_east):
        return jnp.where(
            even,
            pltpu.roll(from_east, cols - 1, 1) * keep_high,
            pltpu.roll(from_west, 1, 1) * keep_low,
        )

    pltpu.make_async_copy(
        near_v.at[pl.ds(0, 8)], near_v.at[pl.ds(0, 8)], recv_sems.at[0]
    ).wait()

    def field(part, low_edge=None, high_edge=None):
        tiles = []
        for i in range(3):
            block = [near_v[i * 3 + j, pl.ds(part * rows, rows), :] for j in range(3)]
            left = block[0] if low_edge is None else block[0] * low_edge
            right = block[2] if high_edge is None else block[2] * high_edge
            tiles.append([block[1], jnp.where(lane < cols // 2, right, left)])
        return tiles

    def shifts(tiles):
        plus = [[pltpu.roll(v, 1, 1) for v in pair] for pair in tiles]
        minus = [[pltpu.roll(v, cols - 1, 1) for v in pair] for pair in tiles]
        below = [[pltpu.roll(v, 1, 0) for v in pair] for pair in tiles]
        above = [[pltpu.roll(v, rows - 1, 0) for v in pair] for pair in tiles]
        result = []
        for i in range(3):
            pair = []
            for j in range(2):
                pair.append(
                    (
                        jnp.where(first_lane, plus[i][1 - j], plus[i][j]),
                        jnp.where(last_lane, minus[i][1 - j], minus[i][j]),
                        jnp.where(first_sub, below[(i + 2) % 3][j], below[i][j]),
                        jnp.where(last_sub, above[(i + 1) % 3][j], above[i][j]),
                    )
                )
            result.append(pair)
        return result

    def add4(four):
        return (four[0] + four[1]) + (four[2] + four[3])

    cells = [(i, j) for i in range(3) for j in range(2)]

    def each(function):
        return [[function(i, j) for j in range(2)] for i in range(3)]

    mask = field(0, keep_low, keep_high)
    mask_shift = shifts(mask)
    degree = each(lambda i, j: mask[i][j] * add4(mask_shift[i][j]))
    diag = field(1)
    on_self = each(lambda i, j: (2.0 / HALF) * (diag[i][j] + degree[i][j] - CENTER))
    on_near = each(lambda i, j: (2.0 / HALF) * mask[i][j])
    mixing_self = 1.0 - 0.2 * degree[1][0]
    mixing_near = 0.2 * m

    kept = [(1, 0), (1, 1), (0, 0), (2, 0)]

    def keep(k, tiles):
        for n, (i, j) in enumerate(kept):
            put(basis_v, k * len(kept) + n, tiles[i][j])

    def twice(tiles):
        moved = shifts(each(lambda i, j: mask[i][j] * tiles[i][j]))
        return each(lambda i, j: on_self[i][j] * tiles[i][j] - on_near[i][j] * add4(moved[i][j]))

    def row_sum(a, b):
        return jnp.sum(a * b, axis=0, keepdims=True)

    now = field(2)
    keep(0, now)
    doubled = twice(now)
    later = each(lambda i, j: 0.5 * doubled[i][j])
    sums = [row_sum(now[1][0], now[1][0]), row_sum(now[1][0], later[1][0])]
    for k in range(1, ITERS):
        keep(k, later)
        doubled = twice(later)
        before = now
        now = later
        later = each(lambda i, j: doubled[i][j] - before[i][j])
        sums.append(row_sum(now[1][0], now[1][0]))
        sums.append(row_sum(now[1][0], later[1][0]))

    row = jnp.zeros((1, cols), jnp.float32)
    for part in range(2 * ITERS // rows):
        stacked = jnp.concatenate(sums[part * rows : (part + 1) * rows], axis=0)
        spread = jnp.broadcast_to(jnp.sum(stacked, axis=1, keepdims=True), (rows, cols))
        row = row + jnp.sum(
            jnp.where(lane == sub + part * rows, spread, 0.0), axis=0, keepdims=True
        )

    def exchange(buffer, index, count, partner, sem):
        for step in range(1, count):
            send(buffer.at[index], buffer.at[index], sem, partner(step))

    def collect(buffer, count, sem):
        part = buffer.at[pl.ds(0, count - 1)]
        pltpu.make_async_copy(part, part, recv_sems.at[sem]).wait()
        values = [buffer[i] for i in range(count)]
        while len(values) > 1:
            values = [
                values[i] + values[i + 1] if i + 1 < len(values) else values[i]
                for i in range(0, len(values), 2)
            ]
        return values[0]

    sum_a[index_a] = row
    exchange(sum_a, index_a, count_a, partner_a, 5)

    for copy in sent_rows:
        copy.wait_recv()
    for copy in sent_cols:
        copy.wait_recv()
    for g in range(1 + tracers // 2):
        put(
            col_v,
            g,
            joined(
                col_recv[0, pl.ds(g * rows, rows), :], col_recv[1, pl.ds(g * rows, rows), :]
            ),
        )

    def four_around(value, below_row, above_row, columns, index):
        held = m * value
        sides = pltpu.roll(columns, cols - 1 - 2 * index, 1)
        return (
            jnp.where(first_lane, sides, pltpu.roll(held, 1, 1)),
            jnp.where(last_lane, sides, pltpu.roll(held, cols - 1, 1)),
            jnp.where(first_sub, below_row, pltpu.roll(held, 1, 0)),
            jnp.where(last_sub, above_row, pltpu.roll(held, rows - 1, 0)),
        )

    def mixing(value, below_row, above_row, columns, index):
        near = add4(four_around(value, below_row, above_row, columns, index))
        return mixing_self * value + mixing_near * near

    copies[4].wait()
    columns_state = tile(col_v, 0)

    def uptake(i, carry):
        for u in range(unroll):
            level = i * unroll + u
            mixed = [
                mixing(
                    tile(state_v, t * levels + level),
                    spread_row(row_recv.at[0], t * levels + level),
                    spread_row(row_recv.at[1], t * levels + level),
                    columns_state,
                    t * levels + level,
                )
                for t in range(2)
            ]
            phyto, iron = jnp.tanh(mixed[0]), mixed[1]
            squared = iron * iron
            inverse = 1.0 / (1.0 + squared)
            factor = -0.8 * tile(active_v, level).astype(jnp.float32)
            q0 = factor * (1.0 - phyto * phyto) * (squared * inverse)
            q1 = factor * phyto * (2.0 * iron) * (inverse * inverse)
            cot = [tile(cot_v, t * levels + level) for t in range(tracers)]
            mixture = functools.reduce(lambda a, b: a + b, [s * v for s, v in zip(STOICH, cot)])
            put(q_v, level, q0)
            put(q_v, levels + level, q1)
            put(g_v, level, cot[0] + q0 * mixture)
            put(g_v, levels + level, cot[1] + q1 * mixture)
        return carry

    lax.fori_loop(0, levels // unroll, uptake, 0)
    qrow_send[0] = q_v[pl.ds(0, planes, stride=rows), :] * m_first
    qrow_send[1] = q_v[pl.ds(rows - 1, planes, stride=rows), :] * m_last
    put(qcol_send, 0, pack(q_v, 0))
    sent_q = [
        send(qrow_send.at[0], qrow_recv.at[1], 7, low),
        send(qrow_send.at[1], qrow_recv.at[0], 8, high),
        send(qcol_send, qcol_recv.at[1], 9, west),
        send(qcol_send, qcol_recv.at[0], 10, east),
    ]

    columns_cot = [tile(col_v, g + 1) for g in range(tracers // 2)]

    def plain(i, carry):
        for u in range(unroll):
            level = i * unroll + u
            for t in range(2, tracers):
                p = t * levels + level
                put(
                    out_v,
                    p,
                    mixing(
                        tile(cot_v, p),
                        spread_row(row_recv.at[0], planes + p),
                        spread_row(row_recv.at[1], planes + p),
                        columns_cot[t // 2],
                        (t % 2) * levels + level,
                    ),
                )
        return carry

    lax.fori_loop(0, levels // unroll, plain, 0)

    sum_b[index_b] = collect(sum_a, count_a, 5)
    exchange(sum_b, index_b, count_b, partner_b, 6)

    for copy in sent_q:
        copy.wait_recv()
    columns_q = joined(qcol_recv[0], qcol_recv[1])
    weighted = functools.reduce(
        lambda a, b: a + b,
        [
            jnp.where(lane < cols // 2, STOICH[2 * g], STOICH[2 * g + 1]) * columns_cot[g]
            for g in range(tracers // 2)
        ],
    )
    columns_g = columns_cot[0] + columns_q * (weighted + pltpu.roll(weighted, cols // 2, 1))
    for side in range(2):
        mixture = functools.reduce(
            lambda a, b: a + b,
            [
                STOICH[t] * row_recv[side, pl.ds(planes + t * levels, levels), :]
                for t in range(tracers)
            ],
        )
        for t in range(2):
            where = pl.ds(planes + t * levels, levels)
            row_send_part = row_recv[side, where, :]
            row_recv[side, where, :] = (
                row_send_part + qrow_recv[side, pl.ds(t * levels, levels), :] * mixture
            )

    def changed(i, carry):
        for u in range(unroll):
            for t in range(2):
                p = t * levels + i * unroll + u
                put(
                    out_v,
                    p,
                    mixing(
                        tile(g_v, p),
                        spread_row(row_recv.at[0], planes + p),
                        spread_row(row_recv.at[1], planes + p),
                        columns_g,
                        p,
                    ),
                )
                q = tile(q_v, p)
                four = four_around(
                    q,
                    spread_row(qrow_recv.at[0], p),
                    spread_row(qrow_recv.at[1], p),
                    columns_q,
                    p,
                )
                put(shift_v, p * 5, (STOICH_LOAD * mixing_self) * q)
                for n in range(4):
                    put(shift_v, p * 5 + 1 + n, (STOICH_LOAD * mixing_near) * four[n])
        return carry

    lax.fori_loop(0, levels // unroll, changed, 0)

    totals = jnp.broadcast_to(collect(sum_b, count_b, 6), (rows, cols))
    inner_sums = []
    for part in range(2 * ITERS // rows):
        chosen = jnp.sum(
            jnp.where(lane == sub + part * rows, totals, 0.0), axis=1, keepdims=True
        )
        chosen = jnp.broadcast_to(chosen, (rows, cols))
        inner_sums += [
            jnp.broadcast_to(chosen[i : i + 1, :], (rows, cols)) for i in range(rows)
        ]
    nu = [inner_sums[0], inner_sums[1]]
    for k in range(1, ITERS):
        nu.append(2.0 * inner_sums[2 * k] - inner_sums[0])
        nu.append(2.0 * inner_sums[2 * k + 1] - inner_sums[1])
    weights, good = moment_solve(nu)

    solved = {}
    for n, cell in enumerate(kept):
        solved[cell] = functools.reduce(
            lambda a, b: a + b,
            [weights[k] * tile(basis_v, k * len(kept) + n) for k in range(ITERS)],
        )
    own = solved[(1, 0)]
    good_ref[0] = jnp.where(good, 1, 0).astype(jnp.int32)[0, 0]
    held = {cell: mask[cell[0]][cell[1]] * solved[cell] for cell in kept}
    around_x = (
        jnp.where(first_lane, pltpu.roll(held[(1, 1)], 1, 1), pltpu.roll(held[(1, 0)], 1, 1)),
        jnp.where(
            last_lane,
            pltpu.roll(held[(1, 1)], cols - 1, 1),
            pltpu.roll(held[(1, 0)], cols - 1, 1),
        ),
        jnp.where(first_sub, pltpu.roll(held[(0, 0)], 1, 0), pltpu.roll(held[(1, 0)], 1, 0)),
        jnp.where(
            last_sub,
            pltpu.roll(held[(2, 0)], rows - 1, 0),
            pltpu.roll(held[(1, 0)], rows - 1, 0),
        ),
    )
    spread_x = mixing_self * own + mixing_near * add4(around_x)

    for n, value in enumerate((own, *around_x, spread_x)):
        put(found_ref, n, value)

    pltpu.make_async_copy(
        near_v.at[pl.ds(0, 8)], near_v.at[pl.ds(0, 8)], send_sems.at[0]
    ).wait()
    for copy in sent_rows + sent_cols + sent_q:
        copy.wait_send()
    for buffer, count, sem in ((sum_a, count_a, 5), (sum_b, count_b, 6)):
        part = buffer.at[pl.ds(0, count - 1)]
        pltpu.make_async_copy(part, part, send_sems.at[sem]).wait()


def final_kernel(levels, base_ref, shift_ref, found_ref, out_hbm, sol_ref, out_v, sems):
    rows = 8

    def tile(ref, index):
        start = index * rows
        if not isinstance(start, int):
            start = pl.multiple_of(start, rows)
        return ref[pl.ds(start, rows), :]

    own = tile(found_ref, 0)
    around_x = [tile(found_ref, 1 + n) for n in range(4)]
    spread_x = tile(found_ref, 5)
    sol_ref[...] = own
    unroll = 8
    written = []
    for t in (2, 3, 4, 5, 0, 1):
        added = LOAD[t] * spread_x

        def finish(i, carry, t=t, added=added):
            for u in range(unroll):
                p = t * levels + i * unroll + u
                value = tile(base_ref, p) + added
                if t < 2:
                    value = value + tile(shift_ref, p * 5) * own
                    for n in range(4):
                        value = value + tile(shift_ref, p * 5 + 1 + n) * around_x[n]
                out_v[pl.ds(pl.multiple_of(p * rows, rows), rows), :] = value
            return carry

        lax.fori_loop(0, levels // unroll, finish, 0)
        where = pl.ds(t * levels * rows, levels * rows)
        copy = pltpu.make_async_copy(out_v.at[where], out_hbm.at[where], sems.at[t])
        copy.start()
        written.append(copy)
    for copy in written:
        copy.wait()


def on_device(state, cotangent, active, wet, surface_diag):
    tracers, levels, rows, cols = state.shape
    lon_count, lat_count = lax.axis_size("lon"), lax.axis_size("lat")
    total = tracers * levels
    planes = 2 * levels
    inner = min(8, lon_count)
    f32 = jnp.float32
    anywhere = pl.BlockSpec(memory_space=pl.ANY)
    vmem = pl.BlockSpec(memory_space=pltpu.VMEM)

    def in_place(array):
        return pltpu.with_memory_space_constraint(array, pltpu.HBM)

    base, shift, found, good = pl.pallas_call(
        functools.partial(fused_kernel, lon_count, lat_count, levels),
        out_shape=(
            jax.ShapeDtypeStruct((total * rows, cols), f32),
            jax.ShapeDtypeStruct((planes * 5 * rows, cols), f32),
            jax.ShapeDtypeStruct((7 * rows, cols), f32),
            jax.ShapeDtypeStruct((1,), jnp.int32),
        ),
        in_specs=[pl.BlockSpec(memory_space=pltpu.HBM)] * 5,
        out_specs=(vmem, vmem, vmem, pl.BlockSpec(memory_space=pltpu.SMEM)),
        scratch_shapes=[
            pltpu.VMEM((planes * rows, cols), f32),
            pltpu.VMEM((total * rows, cols), f32),
            pltpu.VMEM((levels * rows, cols), jnp.int32),
            pltpu.VMEM((rows, cols), jnp.int32),
            pltpu.VMEM((rows, cols), f32),
            pltpu.VMEM((planes * rows, cols), f32),
            pltpu.VMEM((planes * rows, cols), f32),
            pltpu.VMEM((ITERS * 4 * rows, cols), f32),
            pltpu.VMEM((9, 3 * rows, cols), f32),
            pltpu.VMEM((2, planes + total, cols), f32),
            pltpu.VMEM((2, planes + total, cols), f32),
            pltpu.VMEM((2, planes, cols), f32),
            pltpu.VMEM((2, planes, cols), f32),
            pltpu.VMEM(((1 + tracers // 2) * rows, cols), f32),
            pltpu.VMEM((2, (1 + tracers // 2) * rows, cols), f32),
            pltpu.VMEM((rows, cols), f32),
            pltpu.VMEM((2, rows, cols), f32),
            pltpu.VMEM(((1 + tracers // 2) * rows, cols), f32),
            pltpu.VMEM((2 * (lon_count // inner), 1, cols), f32),
            pltpu.VMEM(((inner // 2) * lat_count, 1, cols), f32),
            pltpu.SemaphoreType.DMA((5,)),
            pltpu.SemaphoreType.DMA((11,)),
            pltpu.SemaphoreType.DMA((11,)),
        ],
        compiler_params=pltpu.CompilerParams(
            collective_id=0, has_side_effects=True, vmem_limit_bytes=32 * 1024 * 1024
        ),
        name="fused_step",
    )(
        in_place(state.reshape(total * rows, cols)),
        in_place(cotangent.reshape(total * rows, cols)),
        in_place(active.reshape(levels * rows, cols)),
        in_place(wet),
        in_place(surface_diag),
    )
    found = lax.cond(
        good[0] > 0, lambda found, *_: found, step_by_step, found, wet, surface_diag
    )
    out, sol = pl.pallas_call(
        functools.partial(final_kernel, levels),
        out_shape=(
            jax.ShapeDtypeStruct((total * rows, cols), f32),
            jax.ShapeDtypeStruct((rows, cols), f32),
        ),
        in_specs=[vmem] * 3,
        out_specs=(anywhere, vmem),
        scratch_shapes=[
            pltpu.VMEM((total * rows, cols), f32),
            pltpu.SemaphoreType.DMA((tracers,)),
        ],
        compiler_params=pltpu.CompilerParams(vmem_limit_bytes=32 * 1024 * 1024),
        name="final_step",
    )(base, shift, found)
    return out.reshape(state.shape), sol


def solution(mesh):
    return jax.shard_map(
        on_device,
        mesh=mesh,
        in_specs=(
            P(None, None, "lon", "lat"),
            P(None, None, "lon", "lat"),
            P(None, "lon", "lat"),
            P("lon", "lat"),
            P("lon", "lat"),
        ),
        out_specs=(P(None, None, "lon", "lat"), P("lon", "lat")),
        check_vma=False,
    )
```

```python
import functools

import jax
import jax.numpy as jnp
from jax import lax
from jax.experimental import pallas as pl
from jax.experimental.pallas import tpu as pltpu
from jax.sharding import PartitionSpec as P

ITERS = 8


GRAV = (0.5, 0.4, -0.3, 0.2, 0.3, -0.4)
LOAD = (0.3, -0.2, 0.25, 0.15, -0.1, 0.2)
STOICH = (1.0, 0.5, -1.1, 0.3, 0.8, -0.6)
STOICH_LOAD = sum(s * w for s, w in zip(STOICH, LOAD))

CENTER = 4.11
HALF = 4.09
CONDITION = 1.0e5

MESH = pl.DeviceIdType.MESH


def with_halo(block, sides, width):
    for axis, dim in sides:
        count = lax.axis_size(axis)
        forward = [(i, i + 1) for i in range(count - 1)]
        forward.append((count - 1, 0))
        backward = [(target, source) for source, target in forward]
        low = lax.ppermute(
            lax.slice_in_dim(block, block.shape[dim] - width, None, axis=dim), axis, forward
        )
        high = lax.ppermute(lax.slice_in_dim(block, 0, width, axis=dim), axis, backward)
        block = jnp.concatenate([low, block, high], axis=dim)
    return block


def stencil(padded, mpad):
    center = padded[..., 1:-1, 1:-1]
    m = mpad[1:-1, 1:-1]
    total = m * mpad[2:, 1:-1] * (padded[..., 2:, 1:-1] - center)
    total = total + m * mpad[:-2, 1:-1] * (padded[..., :-2, 1:-1] - center)
    total = total + m * mpad[1:-1, 2:] * (padded[..., 1:-1, 2:] - center)
    total = total + m * mpad[1:-1, :-2] * (padded[..., 1:-1, :-2] - center)
    return total


def surface_operator(field, surface_diag, mpad):
    padded = with_halo(field, (("lon", 0), ("lat", 1)), 1)
    return surface_diag * field - stencil(padded, mpad)


def squares(residual):
    return lax.psum(jnp.sum(residual * residual), ("lon", "lat"))


def step_by_step(found, wet, surface_diag):
    rows, cols = wet.shape
    forcing = found[6 * rows :]
    mpad = with_halo(wet.astype(jnp.float32), (("lon", 0), ("lat", 1)), 1)
    lat_id = lax.axis_index("lat")
    lat_count = lax.axis_size("lat")
    edge = jnp.arange(cols + 2, dtype=jnp.int32)
    keep = jnp.where((edge == 0) & (lat_id == 0), 0.0, 1.0)
    keep = jnp.where((edge == cols + 1) & (lat_id == lat_count - 1), 0.0, keep).astype(jnp.float32)
    mpad = mpad * keep[None, :]

    def iteration(_, carry):
        total, residual, direction, norm_now = carry
        image = surface_operator(direction, surface_diag, mpad)
        alpha = norm_now / lax.psum(jnp.sum(direction * image), ("lon", "lat"))
        total = total + alpha * direction
        residual = residual - alpha * image
        norm_next = squares(residual)
        direction = residual + norm_next / norm_now * direction
        return total, residual, direction, norm_next

    total, _, _, _ = lax.fori_loop(
        0, ITERS, iteration, (jnp.zeros_like(forcing), forcing, forcing, squares(forcing))
    )
    padded = with_halo(total, (("lon", 0), ("lat", 1)), 1)
    spread = total + 0.2 * stencil(padded, mpad)
    held = mpad * padded
    return jnp.concatenate(
        [
            total,
            held[1:-1, :-2],
            held[1:-1, 2:],
            held[:-2, 1:-1],
            held[2:, 1:-1],
            spread,
            forcing,
        ],
        axis=0,
    )


def moment_solve(nu):
    gamma = 2.0 * CENTER / HALF
    zero = jnp.zeros_like(nu[0])
    size = ITERS + 1
    res, dirn = dict(enumerate(nu)), dict(enumerate(nu))
    r = [zero + 1.0] + [None] * (size - 1)
    d = [zero + 1.0] + [None] * (size - 1)
    x = [None] * size
    rr = nu[0]
    condition = zero
    least = rr
    for k in range(ITERS):
        top = 2 * ITERS - 1 - k
        image = {
            l: gamma * dirn[l] + (dirn[l + 1] + dirn[abs(l - 1)]) for l in range(k, top)
        }
        curvature = d[k] * image[k]
        inverse = 1.0 / curvature
        alpha = rr * inverse
        bulk = functools.reduce(lambda a, b: a + b, [jnp.abs(d[l]) for l in range(k + 1)])
        condition = condition + bulk * bulk * inverse
        least = jnp.minimum(least, curvature)
        for l in range(k + 1):
            step = alpha * d[l]
            x[l] = step if x[l] is None else x[l] + step
        if k == ITERS - 1:
            break
        for j in range(k + 2):
            terms = []
            if j > 0:
                terms.append(d[j - 1] * 2.0 if j == 1 else d[j - 1])
            if j + 1 <= k:
                terms.append(d[j + 1])
            if j <= k:
                terms.append(gamma * d[j])
            moved = alpha * functools.reduce(lambda a, b: a + b, terms)
            r[j] = -moved if r[j] is None else r[j] - moved
        res = {l: res[l] - alpha * image[l] for l in range(k + 1, top)}
        rr_next = r[k + 1] * res[k + 1]
        least = jnp.minimum(least, rr_next)
        beta = rr_next / rr
        d = [
            None if r[l] is None else (r[l] if d[l] is None else r[l] + beta * d[l])
            for l in range(size)
        ]
        new = {l: res[l] + beta * dirn[l] for l in range(k + 1, top)}
        new[k] = beta * dirn[k]
        dirn = new
        rr = rr_next
    good = (condition * nu[0] < CONDITION / 4.0) & (least > 0.0)
    return [v * (2.0 / HALF) for v in x[:ITERS]], good


def fused_kernel(
    lon_count,
    lat_count,
    levels,
    state_hbm,
    cot_hbm,
    active_hbm,
    wet_hbm,
    diag_hbm,
    out_v,
    shift_v,
    found_ref,
    good_ref,
    state_v,
    cot_v,
    active_v,
    wet_v,
    diag_v,
    q_v,
    g_v,
    basis_v,
    near_v,
    strip_send,
    strip_v,
    row_send,
    row_recv,
    qrow_send,
    qrow_recv,
    col_send,
    col_recv,
    qcol_send,
    qcol_recv,
    col_v,
    sum_v,
    in_sems,
    send_sems,
    recv_sems,
    told_sem,
):
    rows, cols = 8, 128
    planes = 2 * levels
    lon = lax.axis_index("lon")
    lat = lax.axis_index("lat")
    inner = min(8, lon_count)
    lines = lon_count // inner
    z, pos = lon // inner, lax.rem(lon, inner)

    copies = [
        pltpu.make_async_copy(src, dst, in_sems.at[i])
        for i, (src, dst) in enumerate(
            (
                (wet_hbm, wet_v),
                (diag_hbm, diag_v),
                (cot_hbm, cot_v),
                (state_hbm.at[pl.ds(0, planes * rows)], state_v),
                (active_hbm, active_v),
            )
        )
    ]
    for copy in copies:
        copy.start()

    def member(dz, place, dlat):
        return (
            lax.rem(z + (dz + lines), lines) * inner + place,
            lax.rem(lat + (dlat + lat_count), lat_count),
        )

    def place(step):
        return lax.rem(pos + step, inner)

    sharers = lines * lat_count
    index = z * lat_count + lat

    def sharer(step):
        j = lax.rem(index + step, sharers)
        return ((j // lat_count) * inner + pos, lax.rem(j, lat_count))

    steps = sorted(range(1, sharers), key=lambda s: abs(2 * s - sharers))
    reach = (lines // 2 + 1) // 2
    near = [
        member(dz, pos, dlat)
        for dz in sorted({d % lines for d in range(-reach, reach + 1)})
        for dlat in range(lat_count)
        if (dz, dlat) != (0, 0)
    ]
    partners = list(near)
    partners += [member(1, 0, d) for d in (-1, 0, 1)]
    partners += [member(-1, inner - 1, d) for d in (-1, 0, 1)]
    partners += [member(0, place(s), d) for d in (-1, 0, 1) for s in range(1, inner)]
    barrier = pltpu.get_barrier_semaphore()
    for partner in partners:
        pl.semaphore_signal(barrier, inc=1, device_id=partner, device_id_type=MESH)
    at_end = jnp.where((pos == 0) | (pos == inner - 1), 3 * inner, 0)
    greeted = len(near) + 3 * (inner - 1) + at_end

    lane = lax.broadcasted_iota(jnp.int32, (rows, cols), 1)
    sub = lax.broadcasted_iota(jnp.int32, (rows, cols), 0)
    even = lax.rem(lane, 2) == 0
    first_lane, last_lane = lane == 0, lane == cols - 1
    first_sub, last_sub = sub == 0, sub == rows - 1
    keep_low = jnp.where(lat == 0, 0.0, 1.0).astype(jnp.float32)
    keep_high = jnp.where(lat == lat_count - 1, 0.0, 1.0).astype(jnp.float32)

    def tile(ref, index):
        start = index * rows
        if not isinstance(start, int):
            start = pl.multiple_of(start, rows)
        return ref[pl.ds(start, rows), :]

    def put(ref, index, value):
        start = index * rows
        if not isinstance(start, int):
            start = pl.multiple_of(start, rows)
        ref[pl.ds(start, rows), :] = value

    def spread_row(ref, index):
        return jnp.broadcast_to(ref[pl.ds(index, 1), :], (rows, cols))

    copies[0].wait()
    copies[1].wait()
    m = wet_v[...].astype(jnp.float32)
    near_v[1 + pos, pl.ds(0, rows), :] = m
    near_v[1 + pos, pl.ds(rows, rows), :] = diag_v[...]
    eighth = lane // 8

    def strip(value, high, half):
        spread = jnp.where(eighth == (cols // 8 - 1 if high else 0), value, 0.0)
        for shift in (8, 16, 32, 64):
            spread = spread + pltpu.roll(spread, shift, 1)
        return jnp.sum(
            jnp.where(eighth + sub == rows - 1 + 8 * half, spread, 0.0), axis=0, keepdims=True
        )

    strip_m = [strip(m, high, 1) for high in range(2)]
    for high in range(2):
        strip_send[high, pl.ds(1, 1), :] = strip(diag_v[...], high, 0)
    copies[2].wait()
    tracers = len(GRAV)
    unroll = 4

    def add_levels(i, acc):
        acc = list(acc)
        for u in range(unroll):
            for t in range(tracers):
                acc[t] = acc[t] + tile(cot_v, t * levels + i * unroll + u)
        return tuple(acc)

    acc = lax.fori_loop(
        0, levels // unroll, add_levels, (jnp.zeros((rows, cols), jnp.float32),) * tracers
    )
    forcing = functools.reduce(lambda a, b: a + b, [g * v for g, v in zip(GRAV, acc)])
    forcing = forcing * (1.0 / levels)
    near_v[1 + pos, pl.ds(2 * rows, rows), :] = forcing
    for high in range(2):
        strip_send[high, pl.ds(0, 1), :] = strip(forcing, high, 0) + strip_m[high]
    put(found_ref, 6, forcing)

    pl.semaphore_wait(barrier, greeted)

    def send(src, dst, sem, device):
        copy = pltpu.make_async_remote_copy(
            src_ref=src,
            dst_ref=dst,
            send_sem=send_sems.at[sem],
            recv_sem=recv_sems.at[sem],
            device_id=device,
            device_id_type=MESH,
        )
        copy.start()
        return copy

    def send_strips(dz, slot):
        for dlat, high in ((-1, 0), (1, 1)):
            for s in range(inner):
                send(
                    strip_send.at[high],
                    strip_v.at[1 - high, slot],
                    5,
                    member(dz, place(s), dlat),
                )

    own_tile = near_v.at[1 + pos]

    @pl.when(pos == inner - 1)
    def _():
        send_strips(1, 0)
        for s in range(inner):
            send(own_tile, near_v.at[0], 0, member(1, s, 0))

    @pl.when(pos == 0)
    def _():
        send_strips(-1, inner + 1)
        for s in range(inner):
            send(own_tile, near_v.at[inner + 1], 0, member(-1, s, 0))

    send_strips(0, 1 + pos)
    for s in range(1, inner):
        send(own_tile, own_tile, 0, member(0, place(s), 0))
    for device in near:
        pl.semaphore_signal(told_sem, inc=1, device_id=device, device_id_type=MESH)

    low = (lax.rem(lon + (lon_count - 1), lon_count), lat)
    high = (lax.rem(lon + 1, lon_count), lat)
    west, east = member(0, pos, -1), member(0, pos, 1)

    copies[3].wait()
    m_first, m_last = m[0:1, :], m[rows - 1 : rows, :]
    total = tracers * levels
    row_send[0, pl.ds(0, planes), :] = state_v[pl.ds(0, planes, stride=rows), :] * m_first
    row_send[1, pl.ds(0, planes), :] = state_v[pl.ds(rows - 1, planes, stride=rows), :] * m_last
    row_send[0, pl.ds(planes, total), :] = cot_v[pl.ds(0, total, stride=rows), :] * m_first
    row_send[1, pl.ds(planes, total), :] = cot_v[pl.ds(rows - 1, total, stride=rows), :] * m_last
    sent_rows = [
        send(row_send.at[0], row_recv.at[1], 1, low),
        send(row_send.at[1], row_recv.at[0], 2, high),
    ]

    m_edges = jnp.where(even, m[:, cols - 1 : cols], m[:, 0:1])
    half = lane // 2
    pack_unroll = 8

    def pack(ref, base):
        def some(i, packed):
            for u in range(pack_unroll):
                p = i * pack_unroll + u
                moved = pltpu.roll(tile(ref, base + p), 2 * p + 1, 1)
                packed = jnp.where(half == p, moved, packed)
            return packed

        packed = lax.fori_loop(
            0, planes // pack_unroll, some, jnp.zeros((rows, cols), jnp.float32)
        )
        return packed * m_edges

    put(col_send, 0, pack(state_v, 0))
    for g in range(tracers // 2):
        put(col_send, g + 1, pack(cot_v, g * planes))
    sent_cols = [
        send(col_send, col_recv.at[1], 3, west),
        send(col_send, col_recv.at[0], 4, east),
    ]

    def joined(from_west, from_east):
        return jnp.where(
            even,
            pltpu.roll(from_east, cols - 1, 1) * keep_high,
            pltpu.roll(from_west, 1, 1) * keep_low,
        )

    span = inner + 2
    pltpu.make_async_copy(
        near_v.at[pl.ds(0, inner + 1)], near_v.at[pl.ds(0, inner + 1)], recv_sems.at[0]
    ).wait()
    pltpu.make_async_copy(strip_v, strip_v, recv_sems.at[5]).wait()

    def unstrip(side, i, line, half):
        spread = jnp.broadcast_to(strip_v[side, i, pl.ds(line, 1), :], (rows, cols))
        start = (0 if side else cols - 8) + half * (cols // 2) - 8 * (rows - 1)
        return pltpu.roll(spread, start % cols, 1, stride=8, stride_axis=0)

    def field(part, line, half):
        return [
            [
                near_v[i, pl.ds(part * rows, rows), :],
                jnp.where(
                    lane < cols // 2, unstrip(1, i, line, half), unstrip(0, i, line, half)
                ),
            ]
            for i in range(span)
        ]

    def shifts(tiles):
        plus = [[pltpu.roll(v, 1, 1) for v in pair] for pair in tiles]
        minus = [[pltpu.roll(v, cols - 1, 1) for v in pair] for pair in tiles]
        below = [[pltpu.roll(v, 1, 0) for v in pair] for pair in tiles]
        above = [[pltpu.roll(v, rows - 1, 0) for v in pair] for pair in tiles]
        result = []
        for i in range(span):
            pair = []
            for j in range(2):
                pair.append(
                    (
                        jnp.where(first_lane, plus[i][1 - j], plus[i][j]),
                        jnp.where(last_lane, minus[i][1 - j], minus[i][j]),
                        jnp.where(first_sub, below[(i + span - 1) % span][j], below[i][j]),
                        jnp.where(last_sub, above[(i + 1) % span][j], above[i][j]),
                    )
                )
            result.append(pair)
        return result

    def add4(four):
        return (four[0] + four[1]) + (four[2] + four[3])

    def each(function):
        return [[function(i, j) for j in range(2)] for i in range(span)]

    def keep(k, tiles):
        for i in range(span):
            for j in range(2):
                put(basis_v, (k * span + i) * 2 + j, tiles[i][j])

    def kept(k, i, j):
        return tile(basis_v, (k * span + i) * 2 + j)

    mask = field(0, 0, 1)
    inside = jnp.where(lane < 8, keep_high, jnp.where(lane >= cols - 8, keep_low, 0.0))
    mask = [[pair[0], pair[1] * inside] for pair in mask]
    mask_shift = shifts(mask)
    degree = each(lambda i, j: mask[i][j] * add4(mask_shift[i][j]))
    diag = field(1, 1, 0)
    on_self = each(lambda i, j: (2.0 / HALF) * (diag[i][j] + degree[i][j] - CENTER))
    on_near = each(lambda i, j: (2.0 / HALF) * mask[i][j])
    keep(ITERS, mask)
    keep(ITERS + 1, degree)
    mixing_self = 1.0 - 0.2 * kept(ITERS + 1, 1 + pos, 0)
    mixing_near = 0.2 * m

    def twice(tiles):
        moved = shifts(each(lambda i, j: mask[i][j] * tiles[i][j]))
        return each(lambda i, j: on_self[i][j] * tiles[i][j] - on_near[i][j] * add4(moved[i][j]))

    def row_sum(a, b):
        products = [a[i][0] * b[i][0] for i in range(1, inner + 1)]
        while len(products) > 1:
            products = [
                products[i] + products[i + 1] if i + 1 < len(products) else products[i]
                for i in range(0, len(products), 2)
            ]
        return jnp.sum(products[0], axis=0, keepdims=True)

    now = field(2, 0, 0)
    keep(0, now)
    doubled = twice(now)
    later = each(lambda i, j: 0.5 * doubled[i][j])
    sums = [row_sum(now, now), row_sum(now, later)]
    for k in range(1, ITERS):
        keep(k, later)
        doubled = twice(later)
        before = now
        now = later
        later = each(lambda i, j: doubled[i][j] - before[i][j])
        sums.append(row_sum(now, now))
        sums.append(row_sum(now, later))

    row = jnp.zeros((1, cols), jnp.float32)
    for part in range(2 * ITERS // rows):
        stacked = jnp.concatenate(sums[part * rows : (part + 1) * rows], axis=0)
        spread = jnp.broadcast_to(jnp.sum(stacked, axis=1, keepdims=True), (rows, cols))
        row = row + jnp.sum(
            jnp.where(lane == sub + part * rows, spread, 0.0), axis=0, keepdims=True
        )

    sum_v[index] = row
    pl.semaphore_wait(told_sem, len(near))
    for s in steps:
        send(sum_v.at[index], sum_v.at[index], 6, sharer(s))

    for copy in sent_rows:
        copy.wait_recv()
    for copy in sent_cols:
        copy.wait_recv()
    for g in range(1 + tracers // 2):
        put(
            col_v,
            g,
            joined(
                col_recv[0, pl.ds(g * rows, rows), :], col_recv[1, pl.ds(g * rows, rows), :]
            ),
        )

    def four_around(value, below_row, above_row, columns, index):
        held = m * value
        sides = pltpu.roll(columns, cols - 1 - 2 * index, 1)
        return (
            jnp.where(first_lane, sides, pltpu.roll(held, 1, 1)),
            jnp.where(last_lane, sides, pltpu.roll(held, cols - 1, 1)),
            jnp.where(first_sub, below_row, pltpu.roll(held, 1, 0)),
            jnp.where(last_sub, above_row, pltpu.roll(held, rows - 1, 0)),
        )

    def mixing(value, below_row, above_row, columns, index):
        near = add4(four_around(value, below_row, above_row, columns, index))
        return mixing_self * value + mixing_near * near

    copies[4].wait()
    columns_state = tile(col_v, 0)

    def uptake(i, carry):
        for u in range(unroll):
            level = i * unroll + u
            mixed = [
                mixing(
                    tile(state_v, t * levels + level),
                    spread_row(row_recv.at[0], t * levels + level),
                    spread_row(row_recv.at[1], t * levels + level),
                    columns_state,
                    t * levels + level,
                )
                for t in range(2)
            ]
            phyto, iron = jnp.tanh(mixed[0]), mixed[1]
            squared = iron * iron
            inverse = 1.0 / (1.0 + squared)
            factor = -0.8 * tile(active_v, level).astype(jnp.float32)
            q0 = factor * (1.0 - phyto * phyto) * (squared * inverse)
            q1 = factor * phyto * (2.0 * iron) * (inverse * inverse)
            cot = [tile(cot_v, t * levels + level) for t in range(tracers)]
            mixture = functools.reduce(lambda a, b: a + b, [s * v for s, v in zip(STOICH, cot)])
            put(q_v, level, q0)
            put(q_v, levels + level, q1)
            put(g_v, level, cot[0] + q0 * mixture)
            put(g_v, levels + level, cot[1] + q1 * mixture)
        return carry

    lax.fori_loop(0, levels // unroll, uptake, 0)
    qrow_send[0] = q_v[pl.ds(0, planes, stride=rows), :] * m_first
    qrow_send[1] = q_v[pl.ds(rows - 1, planes, stride=rows), :] * m_last
    put(qcol_send, 0, pack(q_v, 0))
    sent_q = [
        send(qrow_send.at[0], qrow_recv.at[1], 7, low),
        send(qrow_send.at[1], qrow_recv.at[0], 8, high),
        send(qcol_send, qcol_recv.at[1], 9, west),
        send(qcol_send, qcol_recv.at[0], 10, east),
    ]

    columns_cot = [tile(col_v, g + 1) for g in range(tracers // 2)]

    def plain(i, carry):
        for u in range(unroll):
            level = i * unroll + u
            for t in range(2, tracers):
                p = t * levels + level
                put(
                    out_v,
                    p,
                    mixing(
                        tile(cot_v, p),
                        spread_row(row_recv.at[0], planes + p),
                        spread_row(row_recv.at[1], planes + p),
                        columns_cot[t // 2],
                        (t % 2) * levels + level,
                    ),
                )
        return carry

    lax.fori_loop(0, levels // unroll, plain, 0)

    for copy in sent_q:
        copy.wait_recv()
    columns_q = joined(qcol_recv[0], qcol_recv[1])
    weighted = functools.reduce(
        lambda a, b: a + b,
        [
            jnp.where(lane < cols // 2, STOICH[2 * g], STOICH[2 * g + 1]) * columns_cot[g]
            for g in range(tracers // 2)
        ],
    )
    columns_g = columns_cot[0] + columns_q * (weighted + pltpu.roll(weighted, cols // 2, 1))
    for side in range(2):
        mixture = functools.reduce(
            lambda a, b: a + b,
            [
                STOICH[t] * row_recv[side, pl.ds(planes + t * levels, levels), :]
                for t in range(tracers)
            ],
        )
        for t in range(2):
            where = pl.ds(planes + t * levels, levels)
            row_send_part = row_recv[side, where, :]
            row_recv[side, where, :] = (
                row_send_part + qrow_recv[side, pl.ds(t * levels, levels), :] * mixture
            )

    def changed(i, carry):
        for u in range(unroll):
            for t in range(2):
                p = t * levels + i * unroll + u
                put(
                    out_v,
                    p,
                    mixing(
                        tile(g_v, p),
                        spread_row(row_recv.at[0], planes + p),
                        spread_row(row_recv.at[1], planes + p),
                        columns_g,
                        p,
                    ),
                )
                q = tile(q_v, p)
                four = four_around(
                    q,
                    spread_row(qrow_recv.at[0], p),
                    spread_row(qrow_recv.at[1], p),
                    columns_q,
                    p,
                )
                put(shift_v, p * 5, (STOICH_LOAD * mixing_self) * q)
                for n in range(4):
                    put(shift_v, p * 5 + 1 + n, (STOICH_LOAD * mixing_near) * four[n])
        return carry

    lax.fori_loop(0, levels // unroll, changed, 0)

    others = sum_v.at[pl.ds(0, sharers - 1)]
    pltpu.make_async_copy(others, others, recv_sems.at[6]).wait()
    totals = [sum_v[i] for i in range(sharers)]
    while len(totals) > 1:
        totals = [
            totals[i] + totals[i + 1] if i + 1 < len(totals) else totals[i]
            for i in range(0, len(totals), 2)
        ]
    totals = jnp.broadcast_to(totals[0], (rows, cols))
    inner_sums = []
    for part in range(2 * ITERS // rows):
        chosen = jnp.sum(
            jnp.where(lane == sub + part * rows, totals, 0.0), axis=1, keepdims=True
        )
        chosen = jnp.broadcast_to(chosen, (rows, cols))
        inner_sums += [
            jnp.broadcast_to(chosen[i : i + 1, :], (rows, cols)) for i in range(rows)
        ]
    nu = [inner_sums[0], inner_sums[1]]
    for k in range(1, ITERS):
        nu.append(2.0 * inner_sums[2 * k] - inner_sums[0])
        nu.append(2.0 * inner_sums[2 * k + 1] - inner_sums[1])
    weights, good = moment_solve(nu)

    cells = [(1 + pos, 0), (1 + pos, 1), (pos, 0), (2 + pos, 0)]
    solved = [
        functools.reduce(
            lambda a, b: a + b, [weights[k] * kept(k, i, j) for k in range(ITERS)]
        )
        for i, j in cells
    ]
    own = solved[0]
    good_ref[0] = jnp.where(good, 1, 0).astype(jnp.int32)[0, 0]
    held = [kept(ITERS, i, j) * v for (i, j), v in zip(cells, solved)]
    around_x = (
        jnp.where(first_lane, pltpu.roll(held[1], 1, 1), pltpu.roll(held[0], 1, 1)),
        jnp.where(last_lane, pltpu.roll(held[1], cols - 1, 1), pltpu.roll(held[0], cols - 1, 1)),
        jnp.where(first_sub, pltpu.roll(held[2], 1, 0), pltpu.roll(held[0], 1, 0)),
        jnp.where(last_sub, pltpu.roll(held[3], rows - 1, 0), pltpu.roll(held[0], rows - 1, 0)),
    )
    spread_x = mixing_self * own + mixing_near * add4(around_x)

    for n, value in enumerate((own, *around_x, spread_x)):
        put(found_ref, n, value)

    def left(ref, sem):
        pltpu.make_async_copy(ref, ref, send_sems.at[sem]).wait()

    left(near_v.at[pl.ds(0, inner - 1)], 0)
    left(strip_v.at[:, pl.ds(0, inner)], 5)

    @pl.when((pos == 0) | (pos == inner - 1))
    def _():
        left(near_v.at[pl.ds(0, inner)], 0)
        left(strip_v.at[:, pl.ds(0, inner)], 5)

    for copy in sent_rows + sent_cols + sent_q:
        copy.wait_send()
    left(others, 6)


def final_kernel(levels, base_ref, shift_ref, found_ref, out_hbm, sol_hbm, out_v, sems):
    rows = 8

    def tile(ref, index):
        start = index * rows
        if not isinstance(start, int):
            start = pl.multiple_of(start, rows)
        return ref[pl.ds(start, rows), :]

    own = tile(found_ref, 0)
    around_x = [tile(found_ref, 1 + n) for n in range(4)]
    spread_x = tile(found_ref, 5)
    unroll = 8
    written = [pltpu.make_async_copy(found_ref.at[pl.ds(0, rows)], sol_hbm, sems.at[6])]
    written[0].start()
    for t in (2, 3, 4, 5, 0, 1):
        added = LOAD[t] * spread_x

        def finish(i, carry, t=t, added=added):
            for u in range(unroll):
                p = t * levels + i * unroll + u
                value = tile(base_ref, p) + added
                if t < 2:
                    value = value + tile(shift_ref, p * 5) * own
                    for n in range(4):
                        value = value + tile(shift_ref, p * 5 + 1 + n) * around_x[n]
                out_v[pl.ds(pl.multiple_of(p * rows, rows), rows), :] = value
            return carry

        lax.fori_loop(0, levels // unroll, finish, 0)
        where = pl.ds(t * levels * rows, levels * rows)
        copy = pltpu.make_async_copy(out_v.at[where], out_hbm.at[where], sems.at[t])
        copy.start()
        written.append(copy)
    for copy in written:
        copy.wait()


def on_device(state, cotangent, active, wet, surface_diag):
    tracers, levels, rows, cols = state.shape
    lon_count, lat_count = lax.axis_size("lon"), lax.axis_size("lat")
    total = tracers * levels
    planes = 2 * levels
    inner = min(8, lon_count)
    f32 = jnp.float32
    anywhere = pl.BlockSpec(memory_space=pl.ANY)
    vmem = pl.BlockSpec(memory_space=pltpu.VMEM)

    def in_place(array):
        return pltpu.with_memory_space_constraint(array, pltpu.HBM)

    base, shift, found, good = pl.pallas_call(
        functools.partial(fused_kernel, lon_count, lat_count, levels),
        out_shape=(
            jax.ShapeDtypeStruct((total * rows, cols), f32),
            jax.ShapeDtypeStruct((planes * 5 * rows, cols), f32),
            jax.ShapeDtypeStruct((7 * rows, cols), f32),
            pltpu.SMEM((1,), jnp.int32),
        ),
        in_specs=[pl.BlockSpec(memory_space=pltpu.HBM)] * 5,
        out_specs=(vmem, vmem, vmem, pl.BlockSpec(memory_space=pltpu.SMEM)),
        scratch_shapes=[
            pltpu.VMEM((planes * rows, cols), f32),
            pltpu.VMEM((total * rows, cols), f32),
            pltpu.VMEM((levels * rows, cols), jnp.int32),
            pltpu.VMEM((rows, cols), jnp.int32),
            pltpu.VMEM((rows, cols), f32),
            pltpu.VMEM((planes * rows, cols), f32),
            pltpu.VMEM((planes * rows, cols), f32),
            pltpu.VMEM(((ITERS + 2) * (inner + 2) * 2 * rows, cols), f32),
            pltpu.VMEM((inner + 2, 3 * rows, cols), f32),
            pltpu.VMEM((2, 2, cols), f32),
            pltpu.VMEM((2, inner + 2, 2, cols), f32),
            pltpu.VMEM((2, planes + total, cols), f32),
            pltpu.VMEM((2, planes + total, cols), f32),
            pltpu.VMEM((2, planes, cols), f32),
            pltpu.VMEM((2, planes, cols), f32),
            pltpu.VMEM(((1 + tracers // 2) * rows, cols), f32),
            pltpu.VMEM((2, (1 + tracers // 2) * rows, cols), f32),
            pltpu.VMEM((rows, cols), f32),
            pltpu.VMEM((2, rows, cols), f32),
            pltpu.VMEM(((1 + tracers // 2) * rows, cols), f32),
            pltpu.VMEM(((lon_count // inner) * lat_count, 1, cols), f32),
            pltpu.SemaphoreType.DMA((5,)),
            pltpu.SemaphoreType.DMA((11,)),
            pltpu.SemaphoreType.DMA((11,)),
            pltpu.SemaphoreType.REGULAR,
        ],
        compiler_params=pltpu.CompilerParams(
            collective_id=0, has_side_effects=True, vmem_limit_bytes=32 * 1024 * 1024
        ),
        name="fused_step",
    )(
        in_place(state.reshape(total * rows, cols)),
        in_place(cotangent.reshape(total * rows, cols)),
        in_place(active.reshape(levels * rows, cols)),
        in_place(wet),
        in_place(surface_diag),
    )
    found = lax.cond(
        good[0] > 0, lambda found, *_: found, step_by_step, found, wet, surface_diag
    )
    out, sol = pl.pallas_call(
        functools.partial(final_kernel, levels),
        out_shape=(
            jax.ShapeDtypeStruct((total * rows, cols), f32),
            jax.ShapeDtypeStruct((rows, cols), f32),
        ),
        in_specs=[vmem] * 3,
        out_specs=(anywhere, anywhere),
        scratch_shapes=[
            pltpu.VMEM((total * rows, cols), f32),
            pltpu.SemaphoreType.DMA((tracers + 1,)),
        ],
        compiler_params=pltpu.CompilerParams(vmem_limit_bytes=32 * 1024 * 1024),
        name="final_step",
    )(base, shift, found)
    return out.reshape(state.shape), sol


def solution(mesh):
    return jax.shard_map(
        on_device,
        mesh=mesh,
        in_specs=(
            P(None, None, "lon", "lat"),
            P(None, None, "lon", "lat"),
            P(None, "lon", "lat"),
            P("lon", "lat"),
            P("lon", "lat"),
        ),
        out_specs=(P(None, None, "lon", "lat"), P("lon", "lat")),
        check_vma=False,
    )
```

```python
import functools

import jax
import jax.numpy as jnp
from jax import lax
from jax.experimental import pallas as pl
from jax.experimental.pallas import tpu as pltpu
from jax.sharding import PartitionSpec as P

ITERS = 8


GRAV = (0.5, 0.4, -0.3, 0.2, 0.3, -0.4)
LOAD = (0.3, -0.2, 0.25, 0.15, -0.1, 0.2)
STOICH = (1.0, 0.5, -1.1, 0.3, 0.8, -0.6)
STOICH_LOAD = sum(s * w for s, w in zip(STOICH, LOAD))

CENTER = 4.11
HALF = 4.09
CONDITION = 1.0e5

MESH = pl.DeviceIdType.MESH


def with_halo(block, sides, width):
    for axis, dim in sides:
        count = lax.axis_size(axis)
        forward = [(i, i + 1) for i in range(count - 1)]
        forward.append((count - 1, 0))
        backward = [(target, source) for source, target in forward]
        low = lax.ppermute(
            lax.slice_in_dim(block, block.shape[dim] - width, None, axis=dim), axis, forward
        )
        high = lax.ppermute(lax.slice_in_dim(block, 0, width, axis=dim), axis, backward)
        block = jnp.concatenate([low, block, high], axis=dim)
    return block


def stencil(padded, mpad):
    center = padded[..., 1:-1, 1:-1]
    m = mpad[1:-1, 1:-1]
    total = m * mpad[2:, 1:-1] * (padded[..., 2:, 1:-1] - center)
    total = total + m * mpad[:-2, 1:-1] * (padded[..., :-2, 1:-1] - center)
    total = total + m * mpad[1:-1, 2:] * (padded[..., 1:-1, 2:] - center)
    total = total + m * mpad[1:-1, :-2] * (padded[..., 1:-1, :-2] - center)
    return total


def surface_operator(field, surface_diag, mpad):
    padded = with_halo(field, (("lon", 0), ("lat", 1)), 1)
    return surface_diag * field - stencil(padded, mpad)


def squares(residual):
    return lax.psum(jnp.sum(residual * residual), ("lon", "lat"))


def step_by_step(found, wet, surface_diag):
    rows, cols = wet.shape
    forcing = found[6 * rows :]
    mpad = with_halo(wet.astype(jnp.float32), (("lon", 0), ("lat", 1)), 1)
    lat_id = lax.axis_index("lat")
    lat_count = lax.axis_size("lat")
    edge = jnp.arange(cols + 2, dtype=jnp.int32)
    keep = jnp.where((edge == 0) & (lat_id == 0), 0.0, 1.0)
    keep = jnp.where((edge == cols + 1) & (lat_id == lat_count - 1), 0.0, keep).astype(jnp.float32)
    mpad = mpad * keep[None, :]

    def iteration(_, carry):
        total, residual, direction, norm_now = carry
        image = surface_operator(direction, surface_diag, mpad)
        alpha = norm_now / lax.psum(jnp.sum(direction * image), ("lon", "lat"))
        total = total + alpha * direction
        residual = residual - alpha * image
        norm_next = squares(residual)
        direction = residual + norm_next / norm_now * direction
        return total, residual, direction, norm_next

    total, _, _, _ = lax.fori_loop(
        0, ITERS, iteration, (jnp.zeros_like(forcing), forcing, forcing, squares(forcing))
    )
    padded = with_halo(total, (("lon", 0), ("lat", 1)), 1)
    spread = total + 0.2 * stencil(padded, mpad)
    held = mpad * padded
    return jnp.concatenate(
        [
            total,
            held[1:-1, :-2],
            held[1:-1, 2:],
            held[:-2, 1:-1],
            held[2:, 1:-1],
            spread,
            forcing,
        ],
        axis=0,
    )


def moment_solve(nu):
    gamma = 2.0 * CENTER / HALF
    zero = jnp.zeros_like(nu[0])
    size = ITERS + 1
    res, dirn = dict(enumerate(nu)), dict(enumerate(nu))
    r = [zero + 1.0] + [None] * (size - 1)
    d = [zero + 1.0] + [None] * (size - 1)
    x = [None] * size
    rr = nu[0]
    condition = zero
    least = rr
    for k in range(ITERS):
        top = 2 * ITERS - 1 - k
        image = {
            l: gamma * dirn[l] + (dirn[l + 1] + dirn[abs(l - 1)]) for l in range(k, top)
        }
        curvature = d[k] * image[k]
        inverse = 1.0 / curvature
        alpha = rr * inverse
        bulk = functools.reduce(lambda a, b: a + b, [jnp.abs(d[l]) for l in range(k + 1)])
        condition = condition + bulk * bulk * inverse
        least = jnp.minimum(least, curvature)
        for l in range(k + 1):
            step = alpha * d[l]
            x[l] = step if x[l] is None else x[l] + step
        if k == ITERS - 1:
            break
        for j in range(k + 2):
            terms = []
            if j > 0:
                terms.append(d[j - 1] * 2.0 if j == 1 else d[j - 1])
            if j + 1 <= k:
                terms.append(d[j + 1])
            if j <= k:
                terms.append(gamma * d[j])
            moved = alpha * functools.reduce(lambda a, b: a + b, terms)
            r[j] = -moved if r[j] is None else r[j] - moved
        res = {l: res[l] - alpha * image[l] for l in range(k + 1, top)}
        rr_next = r[k + 1] * res[k + 1]
        least = jnp.minimum(least, rr_next)
        beta = rr_next / rr
        d = [
            None if r[l] is None else (r[l] if d[l] is None else r[l] + beta * d[l])
            for l in range(size)
        ]
        new = {l: res[l] + beta * dirn[l] for l in range(k + 1, top)}
        new[k] = beta * dirn[k]
        dirn = new
        rr = rr_next
    good = (condition * nu[0] < CONDITION / 4.0) & (least > 0.0)
    return [v * (2.0 / HALF) for v in x[:ITERS]], good


def fused_kernel(
    lon_count,
    lat_count,
    levels,
    state_hbm,
    cot_hbm,
    active_hbm,
    wet_hbm,
    diag_hbm,
    out_v,
    shift_v,
    found_ref,
    good_ref,
    state_v,
    cot_v,
    active_v,
    wet_v,
    diag_v,
    q_v,
    g_v,
    basis_v,
    self_v,
    sums_v,
    near_v,
    strip_send,
    strip_v,
    row_send,
    row_recv,
    qrow_send,
    qrow_recv,
    col_send,
    col_recv,
    qcol_send,
    qcol_recv,
    col_v,
    sum_v,
    in_sems,
    send_sems,
    recv_sems,
    told_sem,
):
    rows, cols = 8, 128
    planes = 2 * levels
    lon = lax.axis_index("lon")
    lat = lax.axis_index("lat")
    inner = min(8, lon_count)
    lines = lon_count // inner
    z, pos = lon // inner, lax.rem(lon, inner)

    copies = [
        pltpu.make_async_copy(src, dst, in_sems.at[i])
        for i, (src, dst) in enumerate(
            (
                (wet_hbm, wet_v),
                (diag_hbm, diag_v),
                (cot_hbm, cot_v),
                (state_hbm.at[pl.ds(0, planes * rows)], state_v),
                (active_hbm, active_v),
            )
        )
    ]
    for copy in copies:
        copy.start()

    def member(dz, place, dlat):
        return (
            lax.rem(z + (dz + lines), lines) * inner + place,
            lax.rem(lat + (dlat + lat_count), lat_count),
        )

    def place(step):
        return lax.rem(pos + step, inner)

    sharers = lines * lat_count
    index = z * lat_count + lat

    def sharer(step):
        j = lax.rem(index + step, sharers)
        return ((j // lat_count) * inner + pos, lax.rem(j, lat_count))

    steps = sorted(range(1, sharers), key=lambda s: abs(2 * s - sharers))
    reach = (lines // 2 + 1) // 2
    near = [
        member(dz, pos, dlat)
        for dz in sorted({d % lines for d in range(-reach, reach + 1)})
        for dlat in range(lat_count)
        if (dz, dlat) != (0, 0)
    ]
    partners = list(near)
    partners += [member(1, 0, d) for d in (-1, 0, 1)]
    partners += [member(-1, inner - 1, d) for d in (-1, 0, 1)]
    partners += [member(0, place(s), d) for d in (-1, 0, 1) for s in range(1, inner)]
    barrier = pltpu.get_barrier_semaphore()
    for partner in partners:
        pl.semaphore_signal(barrier, inc=1, device_id=partner, device_id_type=MESH)
    at_end = jnp.where((pos == 0) | (pos == inner - 1), 3 * inner, 0)
    greeted = len(near) + 3 * (inner - 1) + at_end

    lane = lax.broadcasted_iota(jnp.int32, (rows, cols), 1)
    sub = lax.broadcasted_iota(jnp.int32, (rows, cols), 0)
    even = lax.rem(lane, 2) == 0
    first_lane, last_lane = lane == 0, lane == cols - 1
    first_sub, last_sub = sub == 0, sub == rows - 1
    keep_low = jnp.where(lat == 0, 0.0, 1.0).astype(jnp.float32)
    keep_high = jnp.where(lat == lat_count - 1, 0.0, 1.0).astype(jnp.float32)

    def tile(ref, index):
        start = index * rows
        if not isinstance(start, int):
            start = pl.multiple_of(start, rows)
        return ref[pl.ds(start, rows), :]

    def put(ref, index, value):
        start = index * rows
        if not isinstance(start, int):
            start = pl.multiple_of(start, rows)
        ref[pl.ds(start, rows), :] = value

    def spread_row(ref, index):
        return jnp.broadcast_to(ref[pl.ds(index, 1), :], (rows, cols))

    copies[0].wait()
    copies[1].wait()
    m = wet_v[...].astype(jnp.float32)
    near_v[1 + pos, pl.ds(0, rows), :] = m
    near_v[1 + pos, pl.ds(rows, rows), :] = diag_v[...]
    eighth = lane // 8

    def strip(value, high, half):
        spread = jnp.where(eighth == (cols // 8 - 1 if high else 0), value, 0.0)
        for shift in (8, 16, 32, 64):
            spread = spread + pltpu.roll(spread, shift, 1)
        return jnp.sum(
            jnp.where(eighth + sub == rows - 1 + 8 * half, spread, 0.0), axis=0, keepdims=True
        )

    strip_m = [strip(m, high, 1) for high in range(2)]
    for high in range(2):
        strip_send[high, pl.ds(1, 1), :] = strip(diag_v[...], high, 0)
    copies[2].wait()
    tracers = len(GRAV)
    unroll = 16

    def add_levels(i, acc):
        acc = list(acc)
        for u in range(unroll):
            for t in range(tracers):
                acc[t] = acc[t] + tile(cot_v, t * levels + i * unroll + u)
        return tuple(acc)

    acc = lax.fori_loop(
        0, levels // unroll, add_levels, (jnp.zeros((rows, cols), jnp.float32),) * tracers
    )
    forcing = functools.reduce(lambda a, b: a + b, [g * v for g, v in zip(GRAV, acc)])
    forcing = forcing * (1.0 / levels)
    near_v[1 + pos, pl.ds(2 * rows, rows), :] = forcing
    for high in range(2):
        strip_send[high, pl.ds(0, 1), :] = strip(forcing, high, 0) + strip_m[high]
    put(found_ref, 6, forcing)

    pl.semaphore_wait(barrier, greeted)

    def send(src, dst, sem, device):
        copy = pltpu.make_async_remote_copy(
            src_ref=src,
            dst_ref=dst,
            send_sem=send_sems.at[sem],
            recv_sem=recv_sems.at[sem],
            device_id=device,
            device_id_type=MESH,
        )
        copy.start()
        return copy

    def send_strips(dz, slot):
        for dlat, high in ((-1, 0), (1, 1)):
            for s in range(inner):
                send(
                    strip_send.at[high],
                    strip_v.at[1 - high, slot],
                    5,
                    member(dz, place(s), dlat),
                )

    own_tile = near_v.at[1 + pos]

    @pl.when(pos == inner - 1)
    def _():
        send_strips(1, 0)
        for s in range(inner):
            send(own_tile, near_v.at[0], 0, member(1, s, 0))

    @pl.when(pos == 0)
    def _():
        send_strips(-1, inner + 1)
        for s in range(inner):
            send(own_tile, near_v.at[inner + 1], 0, member(-1, s, 0))

    send_strips(0, 1 + pos)
    for s in range(1, inner):
        send(own_tile, own_tile, 0, member(0, place(s), 0))
    for device in near:
        pl.semaphore_signal(told_sem, inc=1, device_id=device, device_id_type=MESH)

    low = (lax.rem(lon + (lon_count - 1), lon_count), lat)
    high = (lax.rem(lon + 1, lon_count), lat)
    west, east = member(0, pos, -1), member(0, pos, 1)

    copies[3].wait()
    m_first, m_last = m[0:1, :], m[rows - 1 : rows, :]
    total = tracers * levels
    row_send[0, pl.ds(0, planes), :] = state_v[pl.ds(0, planes, stride=rows), :] * m_first
    row_send[1, pl.ds(0, planes), :] = state_v[pl.ds(rows - 1, planes, stride=rows), :] * m_last
    row_send[0, pl.ds(planes, total), :] = cot_v[pl.ds(0, total, stride=rows), :] * m_first
    row_send[1, pl.ds(planes, total), :] = cot_v[pl.ds(rows - 1, total, stride=rows), :] * m_last
    sent_rows = [
        send(row_send.at[0], row_recv.at[1], 1, low),
        send(row_send.at[1], row_recv.at[0], 2, high),
    ]

    m_edges = jnp.where(even, m[:, cols - 1 : cols], m[:, 0:1])
    half = lane // 2
    pack_unroll = 8

    def pack(ref, base):
        def some(i, packed):
            for u in range(pack_unroll):
                p = i * pack_unroll + u
                moved = pltpu.roll(tile(ref, base + p), 2 * p + 1, 1)
                packed = jnp.where(half == p, moved, packed)
            return packed

        packed = lax.fori_loop(
            0, planes // pack_unroll, some, jnp.zeros((rows, cols), jnp.float32)
        )
        return packed * m_edges

    put(col_send, 0, pack(state_v, 0))
    for g in range(tracers // 2):
        put(col_send, g + 1, pack(cot_v, g * planes))
    sent_cols = [
        send(col_send, col_recv.at[1], 3, west),
        send(col_send, col_recv.at[0], 4, east),
    ]

    def joined(from_west, from_east):
        return jnp.where(
            even,
            pltpu.roll(from_east, cols - 1, 1) * keep_high,
            pltpu.roll(from_west, 1, 1) * keep_low,
        )

    span = inner + 2
    pltpu.make_async_copy(
        near_v.at[pl.ds(0, inner + 1)], near_v.at[pl.ds(0, inner + 1)], recv_sems.at[0]
    ).wait()
    pltpu.make_async_copy(strip_v, strip_v, recv_sems.at[5]).wait()

    def unstrip(side, i, line, half):
        spread = jnp.broadcast_to(strip_v[side, i, pl.ds(line, 1), :], (rows, cols))
        start = (0 if side else cols - 8) + half * (cols // 2) - 8 * (rows - 1)
        return pltpu.roll(spread, start % cols, 1, stride=8, stride_axis=0)

    def field(part, line, half):
        return [
            [
                near_v[i, pl.ds(part * rows, rows), :],
                jnp.where(
                    lane < cols // 2, unstrip(1, i, line, half), unstrip(0, i, line, half)
                ),
            ]
            for i in range(span)
        ]

    def shifts(tiles):
        plus = [[pltpu.roll(v, 1, 1) for v in pair] for pair in tiles]
        minus = [[pltpu.roll(v, cols - 1, 1) for v in pair] for pair in tiles]
        below = [[pltpu.roll(v, 1, 0) for v in pair] for pair in tiles]
        above = [[pltpu.roll(v, rows - 1, 0) for v in pair] for pair in tiles]
        result = []
        for i in range(span):
            pair = []
            for j in range(2):
                pair.append(
                    (
                        jnp.where(first_lane, plus[i][1 - j], plus[i][j]),
                        jnp.where(last_lane, minus[i][1 - j], minus[i][j]),
                        jnp.where(first_sub, below[(i + span - 1) % span][j], below[i][j]),
                        jnp.where(last_sub, above[(i + 1) % span][j], above[i][j]),
                    )
                )
            result.append(pair)
        return result

    def add4(four):
        return (four[0] + four[1]) + (four[2] + four[3])

    def each(function):
        return [[function(i, j) for j in range(2)] for i in range(span)]

    def keep(k, tiles):
        for i in range(span):
            for j in range(2):
                put(basis_v, (k * span + i) * 2 + j, tiles[i][j])

    def kept(k, i, j):
        return tile(basis_v, (k * span + i) * 2 + j)

    mask = field(0, 0, 1)
    inside = jnp.where(lane < 8, keep_high, jnp.where(lane >= cols - 8, keep_low, 0.0))
    mask = [[pair[0], pair[1] * inside] for pair in mask]
    mask_shift = shifts(mask)
    degree = each(lambda i, j: mask[i][j] * add4(mask_shift[i][j]))
    diag = field(1, 1, 0)
    on_self = each(lambda i, j: (2.0 / HALF) * (diag[i][j] + degree[i][j] - CENTER))
    for i in range(span):
        for j in range(2):
            put(self_v, i * 2 + j, on_self[i][j])
    keep(ITERS + 1, mask)
    keep(ITERS + 2, degree)
    mixing_self = 1.0 - 0.2 * kept(ITERS + 2, 1 + pos, 0)
    mixing_near = 0.2 * m

    def twice(k):
        held = each(lambda i, j: kept(ITERS + 1, i, j) * kept(k, i, j))
        moved = shifts(held)
        return each(
            lambda i, j: tile(self_v, i * 2 + j) * kept(k, i, j)
            - (2.0 / HALF) * (kept(ITERS + 1, i, j) * add4(moved[i][j]))
        )

    def row_sum(a, b):
        products = [a[i][0] * b[i][0] for i in range(1, inner + 1)]
        while len(products) > 1:
            products = [
                products[i] + products[i + 1] if i + 1 < len(products) else products[i]
                for i in range(0, len(products), 2)
            ]
        return jnp.sum(products[0], axis=0, keepdims=True)

    now = field(2, 0, 0)
    keep(0, now)
    doubled = twice(0)
    later = each(lambda i, j: 0.5 * doubled[i][j])
    keep(1, later)
    sums_v[0] = row_sum(now, now)
    sums_v[1] = row_sum(now, later)

    def raised(k, carry):
        doubled = twice(k)
        now = each(lambda i, j: kept(k, i, j))
        later = each(lambda i, j: doubled[i][j] - kept(k - 1, i, j))
        keep(k + 1, later)
        sums_v[2 * k] = row_sum(now, now)
        sums_v[2 * k + 1] = row_sum(now, later)
        return carry

    lax.fori_loop(1, ITERS, raised, 0)
    sums = [sums_v[i] for i in range(2 * ITERS)]

    row = jnp.zeros((1, cols), jnp.float32)
    for part in range(2 * ITERS // rows):
        stacked = jnp.concatenate(sums[part * rows : (part + 1) * rows], axis=0)
        spread = jnp.broadcast_to(jnp.sum(stacked, axis=1, keepdims=True), (rows, cols))
        row = row + jnp.sum(
            jnp.where(lane == sub + part * rows, spread, 0.0), axis=0, keepdims=True
        )

    sum_v[index] = row
    pl.semaphore_wait(told_sem, len(near))
    for s in steps:
        send(sum_v.at[index], sum_v.at[index], 6, sharer(s))

    for copy in sent_rows:
        copy.wait_recv()
    for copy in sent_cols:
        copy.wait_recv()
    for g in range(1 + tracers // 2):
        put(
            col_v,
            g,
            joined(
                col_recv[0, pl.ds(g * rows, rows), :], col_recv[1, pl.ds(g * rows, rows), :]
            ),
        )

    def four_around(value, below_row, above_row, columns, index):
        held = m * value
        sides = pltpu.roll(columns, cols - 1 - 2 * index, 1)
        return (
            jnp.where(first_lane, sides, pltpu.roll(held, 1, 1)),
            jnp.where(last_lane, sides, pltpu.roll(held, cols - 1, 1)),
            jnp.where(first_sub, below_row, pltpu.roll(held, 1, 0)),
            jnp.where(last_sub, above_row, pltpu.roll(held, rows - 1, 0)),
        )

    def mixing(value, below_row, above_row, columns, index):
        near = add4(four_around(value, below_row, above_row, columns, index))
        return mixing_self * value + mixing_near * near

    copies[4].wait()
    columns_state = tile(col_v, 0)

    def uptake(i, carry):
        for u in range(unroll):
            level = i * unroll + u
            mixed = [
                mixing(
                    tile(state_v, t * levels + level),
                    spread_row(row_recv.at[0], t * levels + level),
                    spread_row(row_recv.at[1], t * levels + level),
                    columns_state,
                    t * levels + level,
                )
                for t in range(2)
            ]
            phyto, iron = jnp.tanh(mixed[0]), mixed[1]
            squared = iron * iron
            inverse = 1.0 / (1.0 + squared)
            factor = -0.8 * tile(active_v, level).astype(jnp.float32)
            q0 = factor * (1.0 - phyto * phyto) * (squared * inverse)
            q1 = factor * phyto * (2.0 * iron) * (inverse * inverse)
            cot = [tile(cot_v, t * levels + level) for t in range(tracers)]
            mixture = functools.reduce(lambda a, b: a + b, [s * v for s, v in zip(STOICH, cot)])
            put(q_v, level, q0)
            put(q_v, levels + level, q1)
            put(g_v, level, cot[0] + q0 * mixture)
            put(g_v, levels + level, cot[1] + q1 * mixture)
        return carry

    lax.fori_loop(0, levels // unroll, uptake, 0)
    qrow_send[0] = q_v[pl.ds(0, planes, stride=rows), :] * m_first
    qrow_send[1] = q_v[pl.ds(rows - 1, planes, stride=rows), :] * m_last
    put(qcol_send, 0, pack(q_v, 0))
    sent_q = [
        send(qrow_send.at[0], qrow_recv.at[1], 7, low),
        send(qrow_send.at[1], qrow_recv.at[0], 8, high),
        send(qcol_send, qcol_recv.at[1], 9, west),
        send(qcol_send, qcol_recv.at[0], 10, east),
    ]

    columns_cot = [tile(col_v, g + 1) for g in range(tracers // 2)]

    def plain(i, carry):
        for u in range(unroll):
            level = i * unroll + u
            for t in range(2, tracers):
                p = t * levels + level
                put(
                    out_v,
                    p,
                    mixing(
                        tile(cot_v, p),
                        spread_row(row_recv.at[0], planes + p),
                        spread_row(row_recv.at[1], planes + p),
                        columns_cot[t // 2],
                        (t % 2) * levels + level,
                    ),
                )
        return carry

    lax.fori_loop(0, levels // unroll, plain, 0)

    for copy in sent_q:
        copy.wait_recv()
    columns_q = joined(qcol_recv[0], qcol_recv[1])
    weighted = functools.reduce(
        lambda a, b: a + b,
        [
            jnp.where(lane < cols // 2, STOICH[2 * g], STOICH[2 * g + 1]) * columns_cot[g]
            for g in range(tracers // 2)
        ],
    )
    columns_g = columns_cot[0] + columns_q * (weighted + pltpu.roll(weighted, cols // 2, 1))
    for side in range(2):
        mixture = functools.reduce(
            lambda a, b: a + b,
            [
                STOICH[t] * row_recv[side, pl.ds(planes + t * levels, levels), :]
                for t in range(tracers)
            ],
        )
        for t in range(2):
            where = pl.ds(planes + t * levels, levels)
            row_send_part = row_recv[side, where, :]
            row_recv[side, where, :] = (
                row_send_part + qrow_recv[side, pl.ds(t * levels, levels), :] * mixture
            )

    def changed(i, carry):
        for u in range(unroll):
            for t in range(2):
                p = t * levels + i * unroll + u
                put(
                    out_v,
                    p,
                    mixing(
                        tile(g_v, p),
                        spread_row(row_recv.at[0], planes + p),
                        spread_row(row_recv.at[1], planes + p),
                        columns_g,
                        p,
                    ),
                )
                q = tile(q_v, p)
                four = four_around(
                    q,
                    spread_row(qrow_recv.at[0], p),
                    spread_row(qrow_recv.at[1], p),
                    columns_q,
                    p,
                )
                put(shift_v, p * 5, (STOICH_LOAD * mixing_self) * q)
                for n in range(4):
                    put(shift_v, p * 5 + 1 + n, (STOICH_LOAD * mixing_near) * four[n])
        return carry

    lax.fori_loop(0, levels // unroll, changed, 0)

    others = sum_v.at[pl.ds(0, sharers - 1)]
    pltpu.make_async_copy(others, others, recv_sems.at[6]).wait()
    totals = [sum_v[i] for i in range(sharers)]
    while len(totals) > 1:
        totals = [
            totals[i] + totals[i + 1] if i + 1 < len(totals) else totals[i]
            for i in range(0, len(totals), 2)
        ]
    totals = jnp.broadcast_to(totals[0], (rows, cols))
    inner_sums = []
    for part in range(2 * ITERS // rows):
        chosen = jnp.sum(
            jnp.where(lane == sub + part * rows, totals, 0.0), axis=1, keepdims=True
        )
        chosen = jnp.broadcast_to(chosen, (rows, cols))
        inner_sums += [
            jnp.broadcast_to(chosen[i : i + 1, :], (rows, cols)) for i in range(rows)
        ]
    nu = [inner_sums[0], inner_sums[1]]
    for k in range(1, ITERS):
        nu.append(2.0 * inner_sums[2 * k] - inner_sums[0])
        nu.append(2.0 * inner_sums[2 * k + 1] - inner_sums[1])
    weights, good = moment_solve(nu)

    cells = [(1 + pos, 0), (1 + pos, 1), (pos, 0), (2 + pos, 0)]
    solved = [
        functools.reduce(
            lambda a, b: a + b, [weights[k] * kept(k, i, j) for k in range(ITERS)]
        )
        for i, j in cells
    ]
    own = solved[0]
    good_ref[0] = jnp.where(good, 1, 0).astype(jnp.int32)[0, 0]
    held = [kept(ITERS + 1, i, j) * v for (i, j), v in zip(cells, solved)]
    around_x = (
        jnp.where(first_lane, pltpu.roll(held[1], 1, 1), pltpu.roll(held[0], 1, 1)),
        jnp.where(last_lane, pltpu.roll(held[1], cols - 1, 1), pltpu.roll(held[0], cols - 1, 1)),
        jnp.where(first_sub, pltpu.roll(held[2], 1, 0), pltpu.roll(held[0], 1, 0)),
        jnp.where(last_sub, pltpu.roll(held[3], rows - 1, 0), pltpu.roll(held[0], rows - 1, 0)),
    )
    spread_x = mixing_self * own + mixing_near * add4(around_x)

    for n, value in enumerate((own, *around_x, spread_x)):
        put(found_ref, n, value)

    def left(ref, sem):
        pltpu.make_async_copy(ref, ref, send_sems.at[sem]).wait()

    left(near_v.at[pl.ds(0, inner - 1)], 0)
    left(strip_v.at[:, pl.ds(0, inner)], 5)

    @pl.when((pos == 0) | (pos == inner - 1))
    def _():
        left(near_v.at[pl.ds(0, inner)], 0)
        left(strip_v.at[:, pl.ds(0, inner)], 5)

    for copy in sent_rows + sent_cols + sent_q:
        copy.wait_send()
    left(others, 6)


def final_kernel(levels, base_ref, shift_ref, found_ref, out_hbm, sol_hbm, out_v, sems):
    rows = 8

    def tile(ref, index):
        start = index * rows
        if not isinstance(start, int):
            start = pl.multiple_of(start, rows)
        return ref[pl.ds(start, rows), :]

    own = tile(found_ref, 0)
    around_x = [tile(found_ref, 1 + n) for n in range(4)]
    spread_x = tile(found_ref, 5)
    unroll = 8
    written = [pltpu.make_async_copy(found_ref.at[pl.ds(0, rows)], sol_hbm, sems.at[6])]
    written[0].start()
    for t in (2, 3, 4, 5, 0, 1):
        added = LOAD[t] * spread_x

        def finish(i, carry, t=t, added=added):
            for u in range(unroll):
                p = t * levels + i * unroll + u
                value = tile(base_ref, p) + added
                if t < 2:
                    value = value + tile(shift_ref, p * 5) * own
                    for n in range(4):
                        value = value + tile(shift_ref, p * 5 + 1 + n) * around_x[n]
                out_v[pl.ds(pl.multiple_of(p * rows, rows), rows), :] = value
            return carry

        lax.fori_loop(0, levels // unroll, finish, 0)
        where = pl.ds(t * levels * rows, levels * rows)
        copy = pltpu.make_async_copy(out_v.at[where], out_hbm.at[where], sems.at[t])
        copy.start()
        written.append(copy)
    for copy in written:
        copy.wait()


def on_device(state, cotangent, active, wet, surface_diag):
    tracers, levels, rows, cols = state.shape
    lon_count, lat_count = lax.axis_size("lon"), lax.axis_size("lat")
    total = tracers * levels
    planes = 2 * levels
    inner = min(8, lon_count)
    f32 = jnp.float32
    anywhere = pl.BlockSpec(memory_space=pl.ANY)
    vmem = pl.BlockSpec(memory_space=pltpu.VMEM)

    def in_place(array):
        return pltpu.with_memory_space_constraint(array, pltpu.HBM)

    base, shift, found, good = pl.pallas_call(
        functools.partial(fused_kernel, lon_count, lat_count, levels),
        out_shape=(
            jax.ShapeDtypeStruct((total * rows, cols), f32),
            jax.ShapeDtypeStruct((planes * 5 * rows, cols), f32),
            jax.ShapeDtypeStruct((7 * rows, cols), f32),
            pltpu.SMEM((1,), jnp.int32),
        ),
        in_specs=[pl.BlockSpec(memory_space=pltpu.HBM)] * 5,
        out_specs=(vmem, vmem, vmem, pl.BlockSpec(memory_space=pltpu.SMEM)),
        scratch_shapes=[
            pltpu.VMEM((planes * rows, cols), f32),
            pltpu.VMEM((total * rows, cols), f32),
            pltpu.VMEM((levels * rows, cols), jnp.int32),
            pltpu.VMEM((rows, cols), jnp.int32),
            pltpu.VMEM((rows, cols), f32),
            pltpu.VMEM((planes * rows, cols), f32),
            pltpu.VMEM((planes * rows, cols), f32),
            pltpu.VMEM(((ITERS + 3) * (inner + 2) * 2 * rows, cols), f32),
            pltpu.VMEM(((inner + 2) * 2 * rows, cols), f32),
            pltpu.VMEM((2 * ITERS, 1, cols), f32),
            pltpu.VMEM((inner + 2, 3 * rows, cols), f32),
            pltpu.VMEM((2, 2, cols), f32),
            pltpu.VMEM((2, inner + 2, 2, cols), f32),
            pltpu.VMEM((2, planes + total, cols), f32),
            pltpu.VMEM((2, planes + total, cols), f32),
            pltpu.VMEM((2, planes, cols), f32),
            pltpu.VMEM((2, planes, cols), f32),
            pltpu.VMEM(((1 + tracers // 2) * rows, cols), f32),
            pltpu.VMEM((2, (1 + tracers // 2) * rows, cols), f32),
            pltpu.VMEM((rows, cols), f32),
            pltpu.VMEM((2, rows, cols), f32),
            pltpu.VMEM(((1 + tracers // 2) * rows, cols), f32),
            pltpu.VMEM(((lon_count // inner) * lat_count, 1, cols), f32),
            pltpu.SemaphoreType.DMA((5,)),
            pltpu.SemaphoreType.DMA((11,)),
            pltpu.SemaphoreType.DMA((11,)),
            pltpu.SemaphoreType.REGULAR,
        ],
        compiler_params=pltpu.CompilerParams(
            collective_id=0, has_side_effects=True, vmem_limit_bytes=32 * 1024 * 1024
        ),
        name="fused_step",
    )(
        in_place(state.reshape(total * rows, cols)),
        in_place(cotangent.reshape(total * rows, cols)),
        in_place(active.reshape(levels * rows, cols)),
        in_place(wet),
        in_place(surface_diag),
    )
    found = lax.cond(
        good[0] > 0, lambda found, *_: found, step_by_step, found, wet, surface_diag
    )
    out, sol = pl.pallas_call(
        functools.partial(final_kernel, levels),
        out_shape=(
            jax.ShapeDtypeStruct((total * rows, cols), f32),
            jax.ShapeDtypeStruct((rows, cols), f32),
        ),
        in_specs=[vmem] * 3,
        out_specs=(anywhere, anywhere),
        scratch_shapes=[
            pltpu.VMEM((total * rows, cols), f32),
            pltpu.SemaphoreType.DMA((tracers + 1,)),
        ],
        compiler_params=pltpu.CompilerParams(vmem_limit_bytes=32 * 1024 * 1024),
        name="final_step",
    )(base, shift, found)
    return out.reshape(state.shape), sol


def solution(mesh):
    return jax.shard_map(
        on_device,
        mesh=mesh,
        in_specs=(
            P(None, None, "lon", "lat"),
            P(None, None, "lon", "lat"),
            P(None, "lon", "lat"),
            P("lon", "lat"),
            P("lon", "lat"),
        ),
        out_specs=(P(None, None, "lon", "lat"), P("lon", "lat")),
        check_vma=False,
    )
```

```python
import functools

import jax
import jax.numpy as jnp
from jax import lax
from jax.experimental import pallas as pl
from jax.experimental.pallas import tpu as pltpu
from jax.sharding import PartitionSpec as P

ITERS = 8


GRAV = (0.5, 0.4, -0.3, 0.2, 0.3, -0.4)
LOAD = (0.3, -0.2, 0.25, 0.15, -0.1, 0.2)
STOICH = (1.0, 0.5, -1.1, 0.3, 0.8, -0.6)
STOICH_LOAD = sum(s * w for s, w in zip(STOICH, LOAD))

CENTER = 4.11
HALF = 4.09
CONDITION = 1.0e5

MESH = pl.DeviceIdType.MESH


def with_halo(block, sides, width):
    for axis, dim in sides:
        count = lax.axis_size(axis)
        forward = [(i, i + 1) for i in range(count - 1)]
        forward.append((count - 1, 0))
        backward = [(target, source) for source, target in forward]
        low = lax.ppermute(
            lax.slice_in_dim(block, block.shape[dim] - width, None, axis=dim), axis, forward
        )
        high = lax.ppermute(lax.slice_in_dim(block, 0, width, axis=dim), axis, backward)
        block = jnp.concatenate([low, block, high], axis=dim)
    return block


def stencil(padded, mpad):
    center = padded[..., 1:-1, 1:-1]
    m = mpad[1:-1, 1:-1]
    total = m * mpad[2:, 1:-1] * (padded[..., 2:, 1:-1] - center)
    total = total + m * mpad[:-2, 1:-1] * (padded[..., :-2, 1:-1] - center)
    total = total + m * mpad[1:-1, 2:] * (padded[..., 1:-1, 2:] - center)
    total = total + m * mpad[1:-1, :-2] * (padded[..., 1:-1, :-2] - center)
    return total


def surface_operator(field, surface_diag, mpad):
    padded = with_halo(field, (("lon", 0), ("lat", 1)), 1)
    return surface_diag * field - stencil(padded, mpad)


def squares(residual):
    return lax.psum(jnp.sum(residual * residual), ("lon", "lat"))


def step_by_step(found, wet, surface_diag):
    rows, cols = wet.shape
    forcing = found[6 * rows :]
    mpad = with_halo(wet.astype(jnp.float32), (("lon", 0), ("lat", 1)), 1)
    lat_id = lax.axis_index("lat")
    lat_count = lax.axis_size("lat")
    edge = jnp.arange(cols + 2, dtype=jnp.int32)
    keep = jnp.where((edge == 0) & (lat_id == 0), 0.0, 1.0)
    keep = jnp.where((edge == cols + 1) & (lat_id == lat_count - 1), 0.0, keep).astype(jnp.float32)
    mpad = mpad * keep[None, :]

    def iteration(_, carry):
        total, residual, direction, norm_now = carry
        image = surface_operator(direction, surface_diag, mpad)
        alpha = norm_now / lax.psum(jnp.sum(direction * image), ("lon", "lat"))
        total = total + alpha * direction
        residual = residual - alpha * image
        norm_next = squares(residual)
        direction = residual + norm_next / norm_now * direction
        return total, residual, direction, norm_next

    total, _, _, _ = lax.fori_loop(
        0, ITERS, iteration, (jnp.zeros_like(forcing), forcing, forcing, squares(forcing))
    )
    padded = with_halo(total, (("lon", 0), ("lat", 1)), 1)
    spread = total + 0.2 * stencil(padded, mpad)
    held = mpad * padded
    return jnp.concatenate(
        [
            total,
            held[1:-1, :-2],
            held[1:-1, 2:],
            held[:-2, 1:-1],
            held[2:, 1:-1],
            spread,
            forcing,
        ],
        axis=0,
    )


def moment_solve(nu):
    gamma = 2.0 * CENTER / HALF
    zero = jnp.zeros_like(nu[0])
    size = ITERS + 1
    res, dirn = dict(enumerate(nu)), dict(enumerate(nu))
    r = [zero + 1.0] + [None] * (size - 1)
    d = [zero + 1.0] + [None] * (size - 1)
    x = [None] * size
    rr = nu[0]
    condition = zero
    least = rr
    for k in range(ITERS):
        top = 2 * ITERS - 1 - k
        image = {
            l: gamma * dirn[l] + (dirn[l + 1] + dirn[abs(l - 1)]) for l in range(k, top)
        }
        curvature = d[k] * image[k]
        inverse = 1.0 / curvature
        alpha = rr * inverse
        bulk = functools.reduce(lambda a, b: a + b, [jnp.abs(d[l]) for l in range(k + 1)])
        condition = condition + bulk * bulk * inverse
        least = jnp.minimum(least, curvature)
        for l in range(k + 1):
            step = alpha * d[l]
            x[l] = step if x[l] is None else x[l] + step
        if k == ITERS - 1:
            break
        for j in range(k + 2):
            terms = []
            if j > 0:
                terms.append(d[j - 1] * 2.0 if j == 1 else d[j - 1])
            if j + 1 <= k:
                terms.append(d[j + 1])
            if j <= k:
                terms.append(gamma * d[j])
            moved = alpha * functools.reduce(lambda a, b: a + b, terms)
            r[j] = -moved if r[j] is None else r[j] - moved
        res = {l: res[l] - alpha * image[l] for l in range(k + 1, top)}
        rr_next = r[k + 1] * res[k + 1]
        least = jnp.minimum(least, rr_next)
        beta = rr_next / rr
        d = [
            None if r[l] is None else (r[l] if d[l] is None else r[l] + beta * d[l])
            for l in range(size)
        ]
        new = {l: res[l] + beta * dirn[l] for l in range(k + 1, top)}
        new[k] = beta * dirn[k]
        dirn = new
        rr = rr_next
    good = (condition * nu[0] < CONDITION / 4.0) & (least > 0.0)
    return [v * (2.0 / HALF) for v in x[:ITERS]], good


def fused_kernel(
    lon_count,
    lat_count,
    levels,
    state_hbm,
    cot_hbm,
    active_hbm,
    wet_hbm,
    diag_hbm,
    out_v,
    shift_v,
    found_ref,
    good_ref,
    state_v,
    cot_v,
    active_v,
    wet_v,
    diag_v,
    q_v,
    g_v,
    basis_v,
    self_v,
    sums_v,
    near_v,
    strip_send,
    strip_v,
    row_send,
    row_recv,
    qrow_send,
    qrow_recv,
    col_send,
    col_recv,
    qcol_send,
    qcol_recv,
    col_v,
    sum_v,
    in_sems,
    send_sems,
    recv_sems,
    told_sem,
):
    rows, cols = 8, 128
    planes = 2 * levels
    lon = lax.axis_index("lon")
    lat = lax.axis_index("lat")
    inner = min(8, lon_count)
    lines = lon_count // inner
    z, pos = lon // inner, lax.rem(lon, inner)

    copies = [
        pltpu.make_async_copy(src, dst, in_sems.at[i])
        for i, (src, dst) in enumerate(
            (
                (wet_hbm, wet_v),
                (diag_hbm, diag_v),
                (cot_hbm, cot_v),
                (state_hbm.at[pl.ds(0, planes * rows)], state_v),
                (active_hbm, active_v),
            )
        )
    ]
    for copy in copies:
        copy.start()

    def member(dz, place, dlat):
        return (
            lax.rem(z + (dz + lines), lines) * inner + place,
            lax.rem(lat + (dlat + lat_count), lat_count),
        )

    def place(step):
        return lax.rem(pos + step, inner)

    sharers = lines * lat_count
    index = z * lat_count + lat

    def sharer(step):
        j = lax.rem(index + step, sharers)
        return ((j // lat_count) * inner + pos, lax.rem(j, lat_count))

    steps = sorted(range(1, sharers), key=lambda s: abs(2 * s - sharers))
    reach = (lines // 2 + 1) // 2
    lat_reach = (lat_count // 2 + 1) // 2
    near = [
        member(dz, pos, dlat)
        for dz in sorted({d % lines for d in range(-reach, reach + 1)})
        for dlat in sorted({d % lat_count for d in range(-lat_reach, lat_reach + 1)})
        if (dz, dlat) != (0, 0)
    ]
    partners = list(near)
    partners += [member(1, 0, d) for d in (-1, 0, 1)]
    partners += [member(-1, inner - 1, d) for d in (-1, 0, 1)]
    partners += [member(0, place(s), d) for d in (-1, 0, 1) for s in range(1, inner)]
    barrier = pltpu.get_barrier_semaphore()
    for partner in partners:
        pl.semaphore_signal(barrier, inc=1, device_id=partner, device_id_type=MESH)
    at_end = jnp.where((pos == 0) | (pos == inner - 1), 3 * inner, 0)
    greeted = len(near) + 3 * (inner - 1) + at_end

    lane = lax.broadcasted_iota(jnp.int32, (rows, cols), 1)
    sub = lax.broadcasted_iota(jnp.int32, (rows, cols), 0)
    even = lax.rem(lane, 2) == 0
    first_lane, last_lane = lane == 0, lane == cols - 1
    first_sub, last_sub = sub == 0, sub == rows - 1
    keep_low = jnp.where(lat == 0, 0.0, 1.0).astype(jnp.float32)
    keep_high = jnp.where(lat == lat_count - 1, 0.0, 1.0).astype(jnp.float32)

    def tile(ref, index):
        start = index * rows
        if not isinstance(start, int):
            start = pl.multiple_of(start, rows)
        return ref[pl.ds(start, rows), :]

    def put(ref, index, value):
        start = index * rows
        if not isinstance(start, int):
            start = pl.multiple_of(start, rows)
        ref[pl.ds(start, rows), :] = value

    def spread_row(ref, index):
        return jnp.broadcast_to(ref[pl.ds(index, 1), :], (rows, cols))

    copies[0].wait()
    copies[1].wait()
    m = wet_v[...].astype(jnp.float32)
    near_v[1 + pos, pl.ds(0, rows), :] = m
    near_v[1 + pos, pl.ds(rows, rows), :] = diag_v[...]
    eighth = lane // 8

    def strip(value, high, half):
        spread = jnp.where(eighth == (cols // 8 - 1 if high else 0), value, 0.0)
        for shift in (8, 16, 32, 64):
            spread = spread + pltpu.roll(spread, shift, 1)
        return jnp.sum(
            jnp.where(eighth + sub == rows - 1 + 8 * half, spread, 0.0), axis=0, keepdims=True
        )

    strip_m = [strip(m, high, 1) for high in range(2)]
    for high in range(2):
        strip_send[high, pl.ds(1, 1), :] = strip(diag_v[...], high, 0)
    copies[2].wait()
    tracers = len(GRAV)
    unroll = 16

    def add_levels(i, acc):
        acc = list(acc)
        for u in range(unroll):
            for t in range(tracers):
                acc[t] = acc[t] + tile(cot_v, t * levels + i * unroll + u)
        return tuple(acc)

    acc = lax.fori_loop(
        0, levels // unroll, add_levels, (jnp.zeros((rows, cols), jnp.float32),) * tracers
    )
    forcing = functools.reduce(lambda a, b: a + b, [g * v for g, v in zip(GRAV, acc)])
    forcing = forcing * (1.0 / levels)
    near_v[1 + pos, pl.ds(2 * rows, rows), :] = forcing
    for high in range(2):
        strip_send[high, pl.ds(0, 1), :] = strip(forcing, high, 0) + strip_m[high]
    put(found_ref, 6, forcing)

    pl.semaphore_wait(barrier, greeted)

    def send(src, dst, sem, device):
        copy = pltpu.make_async_remote_copy(
            src_ref=src,
            dst_ref=dst,
            send_sem=send_sems.at[sem],
            recv_sem=recv_sems.at[sem],
            device_id=device,
            device_id_type=MESH,
        )
        copy.start()
        return copy

    def send_strips(dz, slot):
        for dlat, high in ((-1, 0), (1, 1)):
            for s in range(inner):
                send(
                    strip_send.at[high],
                    strip_v.at[1 - high, slot],
                    5,
                    member(dz, place(s), dlat),
                )

    own_tile = near_v.at[1 + pos]

    @pl.when(pos == inner - 1)
    def _():
        send_strips(1, 0)
        for s in range(inner):
            send(own_tile, near_v.at[0], 0, member(1, s, 0))

    @pl.when(pos == 0)
    def _():
        send_strips(-1, inner + 1)
        for s in range(inner):
            send(own_tile, near_v.at[inner + 1], 0, member(-1, s, 0))

    send_strips(0, 1 + pos)
    for s in range(1, inner):
        send(own_tile, own_tile, 0, member(0, place(s), 0))
    for device in near:
        pl.semaphore_signal(told_sem, inc=1, device_id=device, device_id_type=MESH)

    low = (lax.rem(lon + (lon_count - 1), lon_count), lat)
    high = (lax.rem(lon + 1, lon_count), lat)
    west, east = member(0, pos, -1), member(0, pos, 1)

    copies[3].wait()
    m_first, m_last = m[0:1, :], m[rows - 1 : rows, :]
    total = tracers * levels
    row_send[0, pl.ds(0, planes), :] = state_v[pl.ds(0, planes, stride=rows), :] * m_first
    row_send[1, pl.ds(0, planes), :] = state_v[pl.ds(rows - 1, planes, stride=rows), :] * m_last
    row_send[0, pl.ds(planes, total), :] = cot_v[pl.ds(0, total, stride=rows), :] * m_first
    row_send[1, pl.ds(planes, total), :] = cot_v[pl.ds(rows - 1, total, stride=rows), :] * m_last
    sent_rows = [
        send(row_send.at[0], row_recv.at[1], 1, low),
        send(row_send.at[1], row_recv.at[0], 2, high),
    ]

    m_edges = jnp.where(even, m[:, cols - 1 : cols], m[:, 0:1])
    half = lane // 2
    pack_unroll = 8

    def pack(ref, base):
        def some(i, packed):
            for u in range(pack_unroll):
                p = i * pack_unroll + u
                moved = pltpu.roll(tile(ref, base + p), 2 * p + 1, 1)
                packed = jnp.where(half == p, moved, packed)
            return packed

        packed = lax.fori_loop(
            0, planes // pack_unroll, some, jnp.zeros((rows, cols), jnp.float32)
        )
        return packed * m_edges

    put(col_send, 0, pack(state_v, 0))
    for g in range(tracers // 2):
        put(col_send, g + 1, pack(cot_v, g * planes))
    sent_cols = [
        send(col_send, col_recv.at[1], 3, west),
        send(col_send, col_recv.at[0], 4, east),
    ]

    def joined(from_west, from_east):
        return jnp.where(
            even,
            pltpu.roll(from_east, cols - 1, 1) * keep_high,
            pltpu.roll(from_west, 1, 1) * keep_low,
        )

    span = inner + 2
    pltpu.make_async_copy(
        near_v.at[pl.ds(0, inner + 1)], near_v.at[pl.ds(0, inner + 1)], recv_sems.at[0]
    ).wait()
    pltpu.make_async_copy(strip_v, strip_v, recv_sems.at[5]).wait()

    def unstrip(side, i, line, half):
        spread = jnp.broadcast_to(strip_v[side, i, pl.ds(line, 1), :], (rows, cols))
        start = (0 if side else cols - 8) + half * (cols // 2) - 8 * (rows - 1)
        return pltpu.roll(spread, start % cols, 1, stride=8, stride_axis=0)

    def field(part, line, half):
        return [
            [
                near_v[i, pl.ds(part * rows, rows), :],
                jnp.where(
                    lane < cols // 2, unstrip(1, i, line, half), unstrip(0, i, line, half)
                ),
            ]
            for i in range(span)
        ]

    def shifts(tiles):
        plus = [[pltpu.roll(v, 1, 1) for v in pair] for pair in tiles]
        minus = [[pltpu.roll(v, cols - 1, 1) for v in pair] for pair in tiles]
        below = [[pltpu.roll(v, 1, 0) for v in pair] for pair in tiles]
        above = [[pltpu.roll(v, rows - 1, 0) for v in pair] for pair in tiles]
        result = []
        for i in range(span):
            pair = []
            for j in range(2):
                pair.append(
                    (
                        jnp.where(first_lane, plus[i][1 - j], plus[i][j]),
                        jnp.where(last_lane, minus[i][1 - j], minus[i][j]),
                        jnp.where(first_sub, below[(i + span - 1) % span][j], below[i][j]),
                        jnp.where(last_sub, above[(i + 1) % span][j], above[i][j]),
                    )
                )
            result.append(pair)
        return result

    def add4(four):
        return (four[0] + four[1]) + (four[2] + four[3])

    def each(function):
        return [[function(i, j) for j in range(2)] for i in range(span)]

    def keep(k, tiles):
        for i in range(span):
            for j in range(2):
                put(basis_v, ((k + 1) * span + i) * 2 + j, tiles[i][j])

    def kept(k, i, j):
        return tile(basis_v, ((k + 1) * span + i) * 2 + j)

    mask = field(0, 0, 1)
    inside = jnp.where(lane < 8, keep_high, jnp.where(lane >= cols - 8, keep_low, 0.0))
    mask = [[pair[0], pair[1] * inside] for pair in mask]
    mask_shift = shifts(mask)
    degree = each(lambda i, j: mask[i][j] * add4(mask_shift[i][j]))
    diag = field(1, 1, 0)
    on_self = each(lambda i, j: (2.0 / HALF) * (diag[i][j] + degree[i][j] - CENTER))
    for i in range(span):
        for j in range(2):
            put(self_v, i * 2 + j, on_self[i][j])
    keep(ITERS + 1, mask)
    keep(ITERS + 2, degree)
    mixing_self = 1.0 - 0.2 * kept(ITERS + 2, 1 + pos, 0)
    mixing_near = 0.2 * m

    def twice(tiles):
        moved = shifts(each(lambda i, j: kept(ITERS + 1, i, j) * tiles[i][j]))
        return each(
            lambda i, j: tile(self_v, i * 2 + j) * tiles[i][j]
            - (2.0 / HALF) * (kept(ITERS + 1, i, j) * add4(moved[i][j]))
        )

    def row_sum(a, b):
        products = [a[i][0] * b[i][0] for i in range(1, inner + 1)]
        while len(products) > 1:
            products = [
                products[i] + products[i + 1] if i + 1 < len(products) else products[i]
                for i in range(0, len(products), 2)
            ]
        return jnp.sum(products[0], axis=0, keepdims=True)

    keep(-1, each(lambda i, j: jnp.zeros((rows, cols), jnp.float32)))
    keep(0, field(2, 0, 0))

    def raised(n, carry):
        k = 2 * n
        share = jnp.where(n == 0, 0.5, 1.0).astype(jnp.float32)
        now = each(lambda i, j: kept(k, i, j))
        doubled = twice(now)
        later = each(lambda i, j: share * doubled[i][j] - kept(k - 1, i, j))
        keep(k + 1, later)
        sums_v[2 * k] = row_sum(now, now)
        sums_v[2 * k + 1] = row_sum(now, later)
        doubled = twice(later)
        last = each(lambda i, j: doubled[i][j] - now[i][j])
        keep(k + 2, last)
        sums_v[2 * k + 2] = row_sum(later, later)
        sums_v[2 * k + 3] = row_sum(later, last)
        return carry

    lax.fori_loop(0, ITERS // 2, raised, 0)
    sums = [sums_v[i] for i in range(2 * ITERS)]

    row = jnp.zeros((1, cols), jnp.float32)
    for part in range(2 * ITERS // rows):
        stacked = jnp.concatenate(sums[part * rows : (part + 1) * rows], axis=0)
        spread = jnp.broadcast_to(jnp.sum(stacked, axis=1, keepdims=True), (rows, cols))
        row = row + jnp.sum(
            jnp.where(lane == sub + part * rows, spread, 0.0), axis=0, keepdims=True
        )

    sum_v[index] = row
    pl.semaphore_wait(told_sem, len(near))
    for s in steps:
        send(sum_v.at[index], sum_v.at[index], 6, sharer(s))

    for copy in sent_rows:
        copy.wait_recv()
    for copy in sent_cols:
        copy.wait_recv()
    for g in range(1 + tracers // 2):
        put(
            col_v,
            g,
            joined(
                col_recv[0, pl.ds(g * rows, rows), :], col_recv[1, pl.ds(g * rows, rows), :]
            ),
        )

    def four_around(value, below_row, above_row, columns, index):
        held = m * value
        sides = pltpu.roll(columns, cols - 1 - 2 * index, 1)
        return (
            jnp.where(first_lane, sides, pltpu.roll(held, 1, 1)),
            jnp.where(last_lane, sides, pltpu.roll(held, cols - 1, 1)),
            jnp.where(first_sub, below_row, pltpu.roll(held, 1, 0)),
            jnp.where(last_sub, above_row, pltpu.roll(held, rows - 1, 0)),
        )

    def mixing(value, below_row, above_row, columns, index):
        near = add4(four_around(value, below_row, above_row, columns, index))
        return mixing_self * value + mixing_near * near

    copies[4].wait()
    columns_state = tile(col_v, 0)

    def uptake(i, carry):
        for u in range(unroll):
            level = i * unroll + u
            mixed = [
                mixing(
                    tile(state_v, t * levels + level),
                    spread_row(row_recv.at[0], t * levels + level),
                    spread_row(row_recv.at[1], t * levels + level),
                    columns_state,
                    t * levels + level,
                )
                for t in range(2)
            ]
            phyto, iron = jnp.tanh(mixed[0]), mixed[1]
            squared = iron * iron
            inverse = 1.0 / (1.0 + squared)
            factor = -0.8 * tile(active_v, level).astype(jnp.float32)
            q0 = factor * (1.0 - phyto * phyto) * (squared * inverse)
            q1 = factor * phyto * (2.0 * iron) * (inverse * inverse)
            cot = [tile(cot_v, t * levels + level) for t in range(tracers)]
            mixture = functools.reduce(lambda a, b: a + b, [s * v for s, v in zip(STOICH, cot)])
            put(q_v, level, q0)
            put(q_v, levels + level, q1)
            put(g_v, level, cot[0] + q0 * mixture)
            put(g_v, levels + level, cot[1] + q1 * mixture)
        return carry

    lax.fori_loop(0, levels // unroll, uptake, 0)
    qrow_send[0] = q_v[pl.ds(0, planes, stride=rows), :] * m_first
    qrow_send[1] = q_v[pl.ds(rows - 1, planes, stride=rows), :] * m_last
    put(qcol_send, 0, pack(q_v, 0))
    sent_q = [
        send(qrow_send.at[0], qrow_recv.at[1], 7, low),
        send(qrow_send.at[1], qrow_recv.at[0], 8, high),
        send(qcol_send, qcol_recv.at[1], 9, west),
        send(qcol_send, qcol_recv.at[0], 10, east),
    ]

    columns_cot = [tile(col_v, g + 1) for g in range(tracers // 2)]

    def plain(i, carry):
        for u in range(4):
            level = i * 4 + u
            for t in range(2, tracers):
                p = t * levels + level
                put(
                    out_v,
                    p,
                    mixing(
                        tile(cot_v, p),
                        spread_row(row_recv.at[0], planes + p),
                        spread_row(row_recv.at[1], planes + p),
                        columns_cot[t // 2],
                        (t % 2) * levels + level,
                    ),
                )
        return carry

    lax.fori_loop(0, levels // 4, plain, 0)

    for copy in sent_q:
        copy.wait_recv()
    columns_q = joined(qcol_recv[0], qcol_recv[1])
    weighted = functools.reduce(
        lambda a, b: a + b,
        [
            jnp.where(lane < cols // 2, STOICH[2 * g], STOICH[2 * g + 1]) * columns_cot[g]
            for g in range(tracers // 2)
        ],
    )
    columns_g = columns_cot[0] + columns_q * (weighted + pltpu.roll(weighted, cols // 2, 1))
    for side in range(2):
        mixture = functools.reduce(
            lambda a, b: a + b,
            [
                STOICH[t] * row_recv[side, pl.ds(planes + t * levels, levels), :]
                for t in range(tracers)
            ],
        )
        for t in range(2):
            where = pl.ds(planes + t * levels, levels)
            row_send_part = row_recv[side, where, :]
            row_recv[side, where, :] = (
                row_send_part + qrow_recv[side, pl.ds(t * levels, levels), :] * mixture
            )

    def changed(i, carry):
        for u in range(unroll):
            for t in range(2):
                p = t * levels + i * unroll + u
                put(
                    out_v,
                    p,
                    mixing(
                        tile(g_v, p),
                        spread_row(row_recv.at[0], planes + p),
                        spread_row(row_recv.at[1], planes + p),
                        columns_g,
                        p,
                    ),
                )
                q = tile(q_v, p)
                four = four_around(
                    q,
                    spread_row(qrow_recv.at[0], p),
                    spread_row(qrow_recv.at[1], p),
                    columns_q,
                    p,
                )
                put(shift_v, p * 5, (STOICH_LOAD * mixing_self) * q)
                for n in range(4):
                    put(shift_v, p * 5 + 1 + n, (STOICH_LOAD * mixing_near) * four[n])
        return carry

    lax.fori_loop(0, levels // unroll, changed, 0)

    others = sum_v.at[pl.ds(0, sharers - 1)]
    pltpu.make_async_copy(others, others, recv_sems.at[6]).wait()
    totals = [sum_v[i] for i in range(sharers)]
    while len(totals) > 1:
        totals = [
            totals[i] + totals[i + 1] if i + 1 < len(totals) else totals[i]
            for i in range(0, len(totals), 2)
        ]
    totals = jnp.broadcast_to(totals[0], (rows, cols))
    inner_sums = []
    for part in range(2 * ITERS // rows):
        chosen = jnp.sum(
            jnp.where(lane == sub + part * rows, totals, 0.0), axis=1, keepdims=True
        )
        chosen = jnp.broadcast_to(chosen, (rows, cols))
        inner_sums += [
            jnp.broadcast_to(chosen[i : i + 1, :], (rows, cols)) for i in range(rows)
        ]
    nu = [inner_sums[0], inner_sums[1]]
    for k in range(1, ITERS):
        nu.append(2.0 * inner_sums[2 * k] - inner_sums[0])
        nu.append(2.0 * inner_sums[2 * k + 1] - inner_sums[1])
    weights, good = moment_solve(nu)

    cells = [(1 + pos, 0), (1 + pos, 1), (pos, 0), (2 + pos, 0)]
    solved = [
        functools.reduce(
            lambda a, b: a + b, [weights[k] * kept(k, i, j) for k in range(ITERS)]
        )
        for i, j in cells
    ]
    own = solved[0]
    good_ref[0] = jnp.where(good, 1, 0).astype(jnp.int32)[0, 0]
    held = [kept(ITERS + 1, i, j) * v for (i, j), v in zip(cells, solved)]
    around_x = (
        jnp.where(first_lane, pltpu.roll(held[1], 1, 1), pltpu.roll(held[0], 1, 1)),
        jnp.where(last_lane, pltpu.roll(held[1], cols - 1, 1), pltpu.roll(held[0], cols - 1, 1)),
        jnp.where(first_sub, pltpu.roll(held[2], 1, 0), pltpu.roll(held[0], 1, 0)),
        jnp.where(last_sub, pltpu.roll(held[3], rows - 1, 0), pltpu.roll(held[0], rows - 1, 0)),
    )
    spread_x = mixing_self * own + mixing_near * add4(around_x)

    for n, value in enumerate((own, *around_x, spread_x)):
        put(found_ref, n, value)

    def left(ref, sem):
        pltpu.make_async_copy(ref, ref, send_sems.at[sem]).wait()

    left(near_v.at[pl.ds(0, inner - 1)], 0)
    left(strip_v.at[:, pl.ds(0, inner)], 5)

    @pl.when((pos == 0) | (pos == inner - 1))
    def _():
        left(near_v.at[pl.ds(0, inner)], 0)
        left(strip_v.at[:, pl.ds(0, inner)], 5)

    for copy in sent_rows + sent_cols + sent_q:
        copy.wait_send()
    left(others, 6)


def final_kernel(levels, base_ref, shift_ref, found_ref, out_hbm, sol_hbm, out_v, sems):
    rows = 8

    def tile(ref, index):
        start = index * rows
        if not isinstance(start, int):
            start = pl.multiple_of(start, rows)
        return ref[pl.ds(start, rows), :]

    own = tile(found_ref, 0)
    around_x = [tile(found_ref, 1 + n) for n in range(4)]
    spread_x = tile(found_ref, 5)
    unroll = 8
    written = [pltpu.make_async_copy(found_ref.at[pl.ds(0, rows)], sol_hbm, sems.at[6])]
    written[0].start()
    for t in (2, 3, 4, 5, 0, 1):
        added = LOAD[t] * spread_x

        def finish(i, carry, t=t, added=added):
            for u in range(unroll):
                p = t * levels + i * unroll + u
                value = tile(base_ref, p) + added
                if t < 2:
                    value = value + tile(shift_ref, p * 5) * own
                    for n in range(4):
                        value = value + tile(shift_ref, p * 5 + 1 + n) * around_x[n]
                out_v[pl.ds(pl.multiple_of(p * rows, rows), rows), :] = value
            return carry

        lax.fori_loop(0, levels // unroll, finish, 0)
        where = pl.ds(t * levels * rows, levels * rows)
        copy = pltpu.make_async_copy(out_v.at[where], out_hbm.at[where], sems.at[t])
        copy.start()
        written.append(copy)
    for copy in written:
        copy.wait()


def on_device(state, cotangent, active, wet, surface_diag):
    tracers, levels, rows, cols = state.shape
    lon_count, lat_count = lax.axis_size("lon"), lax.axis_size("lat")
    total = tracers * levels
    planes = 2 * levels
    inner = min(8, lon_count)
    f32 = jnp.float32
    anywhere = pl.BlockSpec(memory_space=pl.ANY)
    vmem = pl.BlockSpec(memory_space=pltpu.VMEM)

    def in_place(array):
        return pltpu.with_memory_space_constraint(array, pltpu.HBM)

    base, shift, found, good = pl.pallas_call(
        functools.partial(fused_kernel, lon_count, lat_count, levels),
        out_shape=(
            jax.ShapeDtypeStruct((total * rows, cols), f32),
            jax.ShapeDtypeStruct((planes * 5 * rows, cols), f32),
            jax.ShapeDtypeStruct((7 * rows, cols), f32),
            pltpu.SMEM((1,), jnp.int32),
        ),
        in_specs=[pl.BlockSpec(memory_space=pltpu.HBM)] * 5,
        out_specs=(vmem, vmem, vmem, pl.BlockSpec(memory_space=pltpu.SMEM)),
        scratch_shapes=[
            pltpu.VMEM((planes * rows, cols), f32),
            pltpu.VMEM((total * rows, cols), f32),
            pltpu.VMEM((levels * rows, cols), jnp.int32),
            pltpu.VMEM((rows, cols), jnp.int32),
            pltpu.VMEM((rows, cols), f32),
            pltpu.VMEM((planes * rows, cols), f32),
            pltpu.VMEM((planes * rows, cols), f32),
            pltpu.VMEM(((ITERS + 4) * (inner + 2) * 2 * rows, cols), f32),
            pltpu.VMEM(((inner + 2) * 2 * rows, cols), f32),
            pltpu.VMEM((2 * ITERS, 1, cols), f32),
            pltpu.VMEM((inner + 2, 3 * rows, cols), f32),
            pltpu.VMEM((2, 2, cols), f32),
            pltpu.VMEM((2, inner + 2, 2, cols), f32),
            pltpu.VMEM((2, planes + total, cols), f32),
            pltpu.VMEM((2, planes + total, cols), f32),
            pltpu.VMEM((2, planes, cols), f32),
            pltpu.VMEM((2, planes, cols), f32),
            pltpu.VMEM(((1 + tracers // 2) * rows, cols), f32),
            pltpu.VMEM((2, (1 + tracers // 2) * rows, cols), f32),
            pltpu.VMEM((rows, cols), f32),
            pltpu.VMEM((2, rows, cols), f32),
            pltpu.VMEM(((1 + tracers // 2) * rows, cols), f32),
            pltpu.VMEM(((lon_count // inner) * lat_count, 1, cols), f32),
            pltpu.SemaphoreType.DMA((5,)),
            pltpu.SemaphoreType.DMA((11,)),
            pltpu.SemaphoreType.DMA((11,)),
            pltpu.SemaphoreType.REGULAR,
        ],
        compiler_params=pltpu.CompilerParams(
            collective_id=0, has_side_effects=True, vmem_limit_bytes=32 * 1024 * 1024
        ),
        name="fused_step",
    )(
        in_place(state.reshape(total * rows, cols)),
        in_place(cotangent.reshape(total * rows, cols)),
        in_place(active.reshape(levels * rows, cols)),
        in_place(wet),
        in_place(surface_diag),
    )
    found = lax.cond(
        good[0] > 0, lambda found, *_: found, step_by_step, found, wet, surface_diag
    )
    out, sol = pl.pallas_call(
        functools.partial(final_kernel, levels),
        out_shape=(
            jax.ShapeDtypeStruct((total * rows, cols), f32),
            jax.ShapeDtypeStruct((rows, cols), f32),
        ),
        in_specs=[vmem] * 3,
        out_specs=(anywhere, anywhere),
        scratch_shapes=[
            pltpu.VMEM((total * rows, cols), f32),
            pltpu.SemaphoreType.DMA((tracers + 1,)),
        ],
        compiler_params=pltpu.CompilerParams(vmem_limit_bytes=32 * 1024 * 1024),
        name="final_step",
    )(base, shift, found)
    return out.reshape(state.shape), sol


def solution(mesh):
    return jax.shard_map(
        on_device,
        mesh=mesh,
        in_specs=(
            P(None, None, "lon", "lat"),
            P(None, None, "lon", "lat"),
            P(None, "lon", "lat"),
            P("lon", "lat"),
            P("lon", "lat"),
        ),
        out_specs=(P(None, None, "lon", "lat"), P("lon", "lat")),
        check_vma=False,
    )
```
